256 devices in a mesh: pix: 32 (over x, z), head: 8 (over y, core).
Axes of the slice: x: 4, y: 4, z: 8, core: 2. Of those that a mesh axis runs over, the one named last changes fastest.
Arguments:
- query_rows: bfloat16 [65536, 1024], P(('pix', 'head')), may hold values from -28 to 28
- key_rows: bfloat16 [65536, 1024], P(('pix', 'head')), may hold values from -28 to 28
- value_rows: bfloat16 [65536, 1024], P(('pix', 'head')), may hold values from -6 to 6
- out_grad: bfloat16 [65536, 1024], P('pix', 'head'), may hold values from -6 to 6
- boundary_send_blocks: int32 [32, 5, 4], replicated, may hold values from 0 to 31, as said below
- neighbours: int32 [1024, 9], replicated, may hold values from 0 to 51, as said below
- live_count: int32 [1024], replicated, may hold values from 8 to 9
Outputs:
- attended: bfloat16 [65536, 1024], P(('pix', 'head'))
- query_grad: bfloat16 [65536, 1024], P('pix', 'head')
- key_grad: bfloat16 [65536, 1024], P('pix', 'head')
- value_grad: bfloat16 [65536, 1024], P('pix', 'head')
The draws below stay inside these ranges and needn't reach their ends.
Inputs may be any that keep to these rules, and one draw needn't show every extreme that they name: For each range the 20 blocks in boundary_send_blocks[r] are distinct. `neighbours`: slot 0 of a block names the block itself (its place in its range); the entries of a row are distinct. A block that is boundary_send_blocks[r, b, s] names 32 + b * 4 + s in slot 1 and no other entry of 32 or more; every other block names only entries below 32.
All inputs are finite; a program needn't handle non-finite values.
Results may differ from the reference program's by a relative error of at most 0.03.
Values may be sent and summed in bfloat16 or wider, within the bound.
No kernel may reach another device: no remote copies, remote signals or barrier semaphores. Data moves between devices by JAX's collectives and lax.ppermute only.
A program may use at most 128 MiB of HBM per device.

```python
import jax
import jax.numpy as jnp
from jax import lax

HEADS = 16
HD = 64
D = 1024
BLK = 64
NNB = 9
NBLK = 32
LEVELS = 5
SEND = 4
BLOCKS = 1024
PIXELS = 65536
N_PIX = 32


def layout(key):
    ranges = BLOCKS // NBLK
    range_keys = jax.random.split(jax.random.fold_in(key, 11), ranges)
    orders = jax.vmap(lambda subkey: jax.random.permutation(subkey, NBLK))(range_keys).astype(jnp.int32)
    senders = orders[:, :LEVELS * SEND].reshape(ranges, LEVELS, SEND)
    position = jnp.argsort(orders, axis=1).astype(jnp.int32).reshape(-1)
    block_keys = jax.random.split(jax.random.fold_in(key, 12), BLOCKS)
    others = jax.vmap(lambda subkey: jax.random.permutation(subkey, NBLK - 1)[:NNB - 1])(block_keys).astype(jnp.int32)
    local = jnp.arange(BLOCKS, dtype=jnp.int32) % NBLK
    others = (local[:, None] + 1 + others) % NBLK
    sender = position < LEVELS * SEND
    second = jnp.where(sender, NBLK + position, others[:, 0])
    rest = jnp.where(sender[:, None], others[:, :NNB - 2], others[:, 1:])
    rows = jnp.concatenate([local[:, None], second[:, None], rest], axis=1).astype(jnp.int32)
    return (senders, rows)


def draw_boundary_send_blocks(key, part):
    senders, rows = layout(key)
    return senders


def draw_neighbours(key, part):
    senders, rows = layout(key)
    return rows


def draw_live_count(key, part):
    key = jax.random.fold_in(key, 3)
    discarded_rows = jax.random.randint(key, (BLOCKS,), 0, 8) == 0
    return (NNB - discarded_rows.astype(jnp.int32)).astype(jnp.int32)


def draw_query_rows(key, part):
    base = key
    key = jax.random.fold_in(base, 5)
    rows = jnp.clip(jax.random.normal(jax.random.fold_in(key, 41), (PIXELS, D)), -6.0, 6.0)
    row_scale = jnp.exp(jax.random.uniform(jax.random.fold_in(key, 42), (PIXELS, 1), minval=jnp.log(0.5), maxval=jnp.log(2.0)))
    result = rows * row_scale
    return result.astype(jnp.bfloat16)


def draw_key_rows(key, part):
    base = key
    key = jax.random.fold_in(base, 6)
    result = jnp.clip(jax.random.normal(jax.random.fold_in(key, 41), (PIXELS, D)), -6.0, 6.0)
    return result.astype(jnp.bfloat16)


def block_levels(own_key, extent, shards, least, top_value):
    gain, own = 1.0, jax.random.fold_in(own_key, 6)
    for dim, parts in shards:
        heights = jnp.exp(jax.random.uniform(jax.random.fold_in(own, dim), (parts,), jnp.float32, least / len(shards), top_value / len(shards)))
        gain = gain * jnp.repeat(heights, extent[dim] // parts).reshape([-1 if axis == dim else 1 for axis in range(len(extent))])
    return gain


def noise(own_key, dims, scale, reach, shards=(), held_as=jnp.bfloat16):
    factor_of = block_levels(own_key, dims, shards, -0.22, 0.18) if shards else 1.0
    values = jax.random.normal(own_key, dims, jnp.float32) * scale * factor_of
    return jnp.minimum(jnp.maximum(values, -reach), reach).astype(held_as)


def setup_inputs(seed: int = 0) -> dict:
    key_of = jax.random.split(jax.random.key(seed), 8)
    query_rows = draw_query_rows(jax.random.fold_in(key_of[7], 71), 0)
    key_rows = draw_key_rows(jax.random.fold_in(key_of[7], 71), 0)
    value_rows = noise(key_of[2], (PIXELS, D), 1.0, 6.0, ((0, 256),))
    out_grad = noise(key_of[3], (PIXELS, D), 1.0, 6.0, ((0, 32), (1, 8)))
    boundary_send_blocks = draw_boundary_send_blocks(jax.random.fold_in(key_of[7], 71), 0)
    neighbours = draw_neighbours(jax.random.fold_in(key_of[7], 71), 0)
    live_count = draw_live_count(jax.random.fold_in(key_of[7], 71), 0)
    return dict(query_rows=query_rows, key_rows=key_rows, value_rows=value_rows, out_grad=out_grad, boundary_send_blocks=boundary_send_blocks, neighbours=neighbours, live_count=live_count)


masked_fill = -1e30


def block_attention(query_block, grad_block, key_ext, value_ext, rows, counts):
    score_scale = HD ** -0.5
    key_group = key_ext[rows].reshape(NBLK, NNB * BLK, HEADS, HD).astype(jnp.float32)
    value_group = value_ext[rows].reshape(NBLK, NNB * BLK, HEADS, HD).astype(jnp.float32)
    query_heads = query_block.reshape(NBLK, BLK, HEADS, HD).astype(jnp.float32)
    grad_heads = grad_block.reshape(NBLK, BLK, HEADS, HD).astype(jnp.float32)
    slot_live = jnp.arange(NNB, dtype=jnp.int32)[None, :] < counts[:, None]
    live_mask = jnp.repeat(slot_live, BLK, axis=1)[:, None, None, :]
    scores = jnp.einsum("iqhd,ikhd->ihqk", query_heads, key_group) * score_scale
    peak = jnp.max(jnp.where(live_mask, scores, masked_fill), axis=-1, keepdims=True)
    summed = jnp.sum(jnp.where(live_mask, jnp.exp(scores - peak), 0.0), axis=-1, keepdims=True)
    log_total = peak + jnp.log(summed)
    weights = jnp.where(live_mask, jnp.exp(scores - log_total), 0.0)
    rounded = weights.astype(jnp.bfloat16).astype(jnp.float32)
    attended = jnp.einsum("ihqk,ikhd->iqhd", rounded, value_group).astype(jnp.bfloat16)
    row_dot = jnp.sum(grad_heads * attended.astype(jnp.float32), axis=-1).transpose(0, 2, 1)[..., None]
    prob_grad = jnp.einsum("iqhd,ikhd->ihqk", grad_heads, value_group)
    score_grad = weights * (prob_grad - row_dot)
    grad_round = score_grad.astype(jnp.bfloat16).astype(jnp.float32)
    query_grad = (jnp.einsum("ihqk,ikhd->iqhd", grad_round, key_group) * score_scale).astype(jnp.bfloat16)
    key_terms = jnp.einsum("ihqk,iqhd->ikhd", grad_round, query_heads) * score_scale
    value_terms = jnp.einsum("ihqk,iqhd->ikhd", rounded, grad_heads)
    extended = NBLK + LEVELS * SEND
    flat_rows = rows.reshape(-1)
    key_acc = jnp.zeros((extended, BLK, D), jnp.float32).at[flat_rows].add(key_terms.reshape(NBLK * NNB, BLK, D))
    value_acc = jnp.zeros((extended, BLK, D), jnp.float32).at[flat_rows].add(value_terms.reshape(NBLK * NNB, BLK, D))
    return attended.reshape(NBLK, BLK, D), query_grad.reshape(NBLK, BLK, D), key_acc, value_acc


def reference(query_rows, key_rows, value_rows, out_grad, boundary_send_blocks, neighbours, live_count):
    query_grid = query_rows.reshape(N_PIX, NBLK, BLK, D)
    key_grid = key_rows.reshape(N_PIX, NBLK, BLK, D)
    value_grid = value_rows.reshape(N_PIX, NBLK, BLK, D)
    grad_grid = out_grad.reshape(N_PIX, NBLK, BLK, D)

    def one_range(range_index):
        key_parts = [key_grid[range_index]]
        value_parts = [value_grid[range_index]]
        for bit_level in range(LEVELS):
            partner = jnp.bitwise_xor(range_index, 1 << bit_level).astype(jnp.int32)
            chosen = boundary_send_blocks[partner, bit_level]
            key_parts.append(key_grid[partner][chosen])
            value_parts.append(value_grid[partner][chosen])
        key_ext = jnp.concatenate(key_parts, axis=0)
        value_ext = jnp.concatenate(value_parts, axis=0)
        start = (range_index * NBLK).astype(jnp.int32)
        rows = lax.dynamic_slice_in_dim(neighbours, start, NBLK, 0)
        counts = lax.dynamic_slice_in_dim(live_count, start, NBLK, 0)
        return block_attention(query_grid[range_index], grad_grid[range_index], key_ext, value_ext, rows, counts)

    attended, query_grad, key_acc, value_acc = lax.map(one_range, jnp.arange(N_PIX, dtype=jnp.int32))
    key_own = key_acc[:, :NBLK]
    value_own = value_acc[:, :NBLK]
    key_recv = key_acc[:, NBLK:].reshape(N_PIX, LEVELS, SEND, BLK, D)
    value_recv = value_acc[:, NBLK:].reshape(N_PIX, LEVELS, SEND, BLK, D)
    index = jnp.arange(N_PIX, dtype=jnp.int32)
    for bit_level in range(LEVELS):
        partner = jnp.bitwise_xor(index, 1 << bit_level).astype(jnp.int32)
        key_own = key_own.at[index[:, None], boundary_send_blocks[:, bit_level]].add(key_recv[partner, bit_level])
        value_own = value_own.at[index[:, None], boundary_send_blocks[:, bit_level]].add(value_recv[partner, bit_level])
    return (attended.reshape(PIXELS, D), query_grad.reshape(PIXELS, D),
            key_own.astype(jnp.bfloat16).reshape(PIXELS, D), value_own.astype(jnp.bfloat16).reshape(PIXELS, D))
```

```python
import functools
import jax
import jax.numpy as jnp
from jax import lax
from jax.experimental import pallas as pl
from jax.experimental.pallas import tpu as pltpu
from jax.sharding import PartitionSpec as P

HD = 64
BLK = 64
NNB = 9
NBLK = 32
LEVELS = 5
SEND = 4
WIDE = 2 * HD
OWN = NBLK * BLK
PART = SEND * BLK
FILL = -1e30
F32 = jnp.float32
BF16 = jnp.bfloat16

VM = pl.BlockSpec(memory_space=pltpu.VMEM)
SM = pl.BlockSpec(memory_space=pltpu.SMEM)


def swapped(block, bit):
    count = lax.axis_size("pix")
    route = [(low, low ^ (1 << bit)) for low in range(count)]
    return lax.ppermute(block, "pix", route)


def rows_of(start):
    return pl.ds(pl.multiple_of(start * BLK, BLK), BLK)


def pick_kernel(sends_ref, own_ref, *out_refs):
    for b in range(LEVELS):
        for s in range(SEND):
            out_refs[b][s * BLK : (s + 1) * BLK, :] = own_ref[rows_of(sends_ref[b, s]), :]


def pick(sends, own):
    return pl.pallas_call(
        pick_kernel,
        out_shape=[jax.ShapeDtypeStruct((PART, 2 * WIDE), BF16)] * LEVELS,
        in_specs=[SM, VM],
        out_specs=[VM] * LEVELS,
        compiler_params=pltpu.CompilerParams(vmem_limit_bytes=16 * 2**20),
        cost_estimate=pl.CostEstimate(flops=0, bytes_accessed=2 * 2**20, transcendentals=0),
        name="pick_boundary",
    )(sends, own)


def attend_block(i, rows_ref, counts_ref, q_ref, g_ref, kv_ref, att_ref, qg_ref, acc_ref):
    at = rows_of(i)
    q = q_ref[at, :] * jnp.array(HD**-0.5, BF16)
    g = g_ref[at, :]
    low = lax.broadcasted_iota(jnp.int32, (BLK, WIDE), 1) < HD
    z = jnp.zeros((BLK, WIDE), BF16)
    both = jnp.concatenate(
        [
            jnp.concatenate([jnp.where(low, q, z), z], 1),
            jnp.concatenate([jnp.where(low, z, q), z], 1),
            jnp.concatenate([z, jnp.where(low, g, z)], 1),
            jnp.concatenate([z, jnp.where(low, z, g)], 1),
        ],
        0,
    )
    starts = [rows_of(rows_ref[i, j]) for j in range(NNB)]
    kv = jnp.concatenate([kv_ref[start, :] for start in starts], 0)
    sd = lax.dot_general(kv, both, (((1,), (1,)), ((), ())), preferred_element_type=F32)
    s = [sd[j * BLK : (j + 1) * BLK, :WIDE] for j in range(NNB)]
    d = [sd[j * BLK : (j + 1) * BLK, WIDE:] for j in range(NNB)]
    s[-1] = jnp.where(counts_ref[i] > NNB - 1, s[-1], FILL)
    peak = functools.reduce(jnp.maximum, s)
    peak = jnp.max(peak, 0, keepdims=True)
    p = [jnp.exp(x - peak) for x in s]
    total = jnp.sum(sum(p[1:], p[0]), 0, keepdims=True)
    dot = [x * y for x, y in zip(p, d)]
    inv = 1.0 / total
    dot = jnp.sum(sum(dot[1:], dot[0]), 0, keepdims=True) * inv
    weights = [x * inv for x in p]
    rounded = jnp.concatenate([x.astype(BF16) for x in weights], 0)
    grads = jnp.concatenate([(x * (y - dot)).astype(BF16) for x, y in zip(weights, d)], 0)
    terms = lax.dot_general(
        jnp.concatenate([grads, rounded], 1), both, (((1,), (0,)), ((), ())), preferred_element_type=F32
    )
    down = (((0,), (0,)), ((), ()))
    qg = lax.dot_general(grads, kv[:, :WIDE], down, preferred_element_type=F32)
    att = lax.dot_general(rounded, kv[:, WIDE:], down, preferred_element_type=F32)
    att_ref[at, :] = jnp.where(low, att[:BLK], att[BLK:]).astype(BF16)
    qg_ref[at, :] = (jnp.where(low, qg[:BLK], qg[BLK:]) * HD**-0.5).astype(BF16)
    for j in range(NNB):
        acc_ref[starts[j], :] += terms[j * BLK : (j + 1) * BLK]


def attend_kernel(unroll, rows_ref, counts_ref, q_ref, g_ref, own_ref, *refs):
    recv_refs = refs[:LEVELS]
    att_ref, qg_ref, acc_out = refs[LEVELS : LEVELS + 3]
    back_refs = refs[LEVELS + 3 : 2 * LEVELS + 3]
    kv_ref, acc_ref = refs[2 * LEVELS + 3 :]
    kv_ref[:OWN, :] = own_ref[...]
    for b in range(LEVELS):
        kv_ref[OWN + b * PART : OWN + (b + 1) * PART, :] = recv_refs[b][...]
    acc_ref[...] = jnp.zeros_like(acc_ref)

    def step(t, carry):
        for u in range(unroll):
            attend_block(t * unroll + u, rows_ref, counts_ref, q_ref, g_ref, kv_ref, att_ref, qg_ref, acc_ref)
        return carry

    lax.fori_loop(0, NBLK // unroll, step, 0)
    acc_out[...] = acc_ref[:OWN, :]
    for b in range(LEVELS):
        back_refs[b][...] = acc_ref[OWN + b * PART : OWN + (b + 1) * PART, :].astype(BF16)


def attend(rows, counts, q, g, own, recv):
    ext = OWN + LEVELS * PART
    return pl.pallas_call(
        functools.partial(attend_kernel, 2),
        out_shape=[
            jax.ShapeDtypeStruct((OWN, WIDE), BF16),
            jax.ShapeDtypeStruct((OWN, WIDE), BF16),
            jax.ShapeDtypeStruct((OWN, 2 * WIDE), F32),
        ]
        + [jax.ShapeDtypeStruct((PART, 2 * WIDE), BF16)] * LEVELS,
        in_specs=[SM, SM] + [VM] * (3 + LEVELS),
        out_specs=[VM] * (3 + LEVELS),
        scratch_shapes=[pltpu.VMEM((ext, 2 * WIDE), BF16), pltpu.VMEM((ext, 2 * WIDE), F32)],
        compiler_params=pltpu.CompilerParams(vmem_limit_bytes=40 * 2**20),
        cost_estimate=pl.CostEstimate(flops=4 * 10**9, bytes_accessed=8 * 2**20, transcendentals=3 * 10**6),
        name="attend_blocks",
    )(rows, counts, q, g, own, *recv)


def join_kernel(sends_ref, acc_ref, *refs):
    arrived_refs = refs[:LEVELS]
    key_ref, value_ref = refs[LEVELS : LEVELS + 2]
    key_ref[...] = acc_ref[:, :WIDE].astype(BF16)
    value_ref[...] = acc_ref[:, WIDE:].astype(BF16)
    for b in range(LEVELS):
        for s in range(SEND):
            at = rows_of(sends_ref[b, s])
            both = acc_ref[at, :] + arrived_refs[b][s * BLK : (s + 1) * BLK, :].astype(F32)
            key_ref[at, :] = both[:, :WIDE].astype(BF16)
            value_ref[at, :] = both[:, WIDE:].astype(BF16)


def join(sends, acc, arrived):
    return pl.pallas_call(
        join_kernel,
        out_shape=[jax.ShapeDtypeStruct((OWN, WIDE), BF16)] * 2,
        in_specs=[SM] + [VM] * (1 + LEVELS),
        out_specs=[VM] * 2,
        compiler_params=pltpu.CompilerParams(vmem_limit_bytes=24 * 2**20),
        cost_estimate=pl.CostEstimate(flops=10**6, bytes_accessed=4 * 2**20, transcendentals=0),
        name="join_gradients",
    )(sends, acc, *arrived)


def body(query_rows, key_rows, value_rows, out_grad, boundary_send_blocks, neighbours, live_count):
    heads = lax.axis_size("head")
    mine = query_rows.shape[0]
    my_range = lax.axis_index("pix")
    sends = lax.dynamic_index_in_dim(boundary_send_blocks, my_range, 0, keepdims=False)
    rows = lax.dynamic_slice_in_dim(neighbours, my_range * NBLK, NBLK, 0)
    counts = lax.dynamic_slice_in_dim(live_count, my_range * NBLK, NBLK, 0)

    def by_head(x):
        return x.reshape(mine, heads, WIDE)

    kv = jnp.concatenate([by_head(key_rows), by_head(value_rows)], axis=2).transpose(1, 0, 2)
    own = lax.all_to_all(kv, "head", 0, 0, tiled=True).reshape(OWN, 2 * WIDE)
    q = lax.all_to_all(by_head(query_rows).transpose(1, 0, 2), "head", 0, 0, tiled=True).reshape(OWN, WIDE)
    outgoing = pick(sends, own)
    recv = [swapped(outgoing[b], b) for b in range(LEVELS)]
    results = attend(rows, counts, q, out_grad, own, recv)
    attended, query_grad, acc = results[:3]
    arrived = [swapped(results[3 + b], b) for b in range(LEVELS)]
    attended = lax.all_to_all(attended.reshape(heads, mine, WIDE), "head", 0, 0, tiled=True)
    attended = attended.transpose(1, 0, 2).reshape(mine, heads * WIDE)
    key_grad, value_grad = join(sends, acc, arrived)
    return attended, query_grad, key_grad, value_grad


def solution(mesh):
    rows = P(("pix", "head"), None)
    split = P("pix", "head")
    return jax.shard_map(
        body,
        mesh=mesh,
        in_specs=(rows, rows, rows, split, P(), P(), P()),
        out_specs=(rows, split, split, split),
        check_vma=False,
    )
```

```python
import functools
import jax
import jax.numpy as jnp
from jax import lax
from jax.experimental import pallas as pl
from jax.experimental.pallas import tpu as pltpu
from jax.sharding import PartitionSpec as P

HD = 64
BLK = 64
NNB = 9
NBLK = 32
LEVELS = 5
SEND = 4
WIDE = 2 * HD
OWN = NBLK * BLK
PART = SEND * BLK
FILL = -1e30
HEAD_DEVICES = 8
OFFSETS = ((1, 0), (3, 0), (1, 1), (3, 1), (2, 0), (2, 1), (0, 1), (0, 0))
F32 = jnp.float32
BF16 = jnp.bfloat16

VM = pl.BlockSpec(memory_space=pltpu.VMEM)
SM = pl.BlockSpec(memory_space=pltpu.SMEM)
HB = pl.BlockSpec(memory_space=pltpu.HBM)


def swapped(block, bit):
    count = lax.axis_size("pix")
    route = [(low, low ^ (1 << bit)) for low in range(count)]
    return lax.ppermute(block, "pix", route)


def rows_of(start):
    return pl.ds(pl.multiple_of(start * BLK, BLK), BLK)


def offset_index(index, steps, core):
    chips = HEAD_DEVICES // 2
    return (index // 2 + steps) % chips * 2 + (index % 2 + core) % 2


def shifted(block, steps, core):
    route = [(i, offset_index(i, steps, core)) for i in range(HEAD_DEVICES)]
    return lax.ppermute(block, "head", route)


def limits(megabytes):
    return pltpu.CompilerParams(vmem_limit_bytes=megabytes * 2**20)


def split_kernel(key_ref, value_ref, *refs):
    parts, sems = refs[:-1], refs[-1]
    me = lax.axis_index("head")
    copies = []
    for t, (steps, core) in enumerate(OFFSETS):
        column = pl.ds(pl.multiple_of(offset_index(me, steps, core) * WIDE, WIDE), WIDE)
        for n, ref in enumerate((key_ref, value_ref)):
            copies.append(
                pltpu.make_async_copy(
                    ref.at[:, column], parts[t].at[:, n * WIDE : (n + 1) * WIDE], sems.at[2 * t + n]
                )
            )
    for copy in copies:
        copy.start()
    for copy in copies:
        copy.wait()


def split(keys, values):
    mine = keys.shape[0]
    return pl.pallas_call(
        split_kernel,
        out_shape=[pltpu.VMEM((mine, 2 * WIDE), BF16)] * HEAD_DEVICES,
        in_specs=[HB] * 2,
        out_specs=[VM] * HEAD_DEVICES,
        scratch_shapes=[pltpu.SemaphoreType.DMA((2 * HEAD_DEVICES,))],
        compiler_params=limits(4),
        cost_estimate=pl.CostEstimate(flops=0, bytes_accessed=2 * 2**20, transcendentals=0),
        name="split_keys_values",
    )(pltpu.with_memory_space_constraint(keys, pltpu.HBM), pltpu.with_memory_space_constraint(values, pltpu.HBM))


def pick_kernel(sends_ref, grad_ref, *refs):
    parts, refs = refs[:HEAD_DEVICES], refs[HEAD_DEVICES:]
    own_ref, near_ref, out_refs, sem = refs[0], refs[1], refs[2:-1], refs[-1]
    copy = pltpu.make_async_copy(grad_ref, near_ref, sem)
    copy.start()
    me = lax.axis_index("head")
    mine = OWN // HEAD_DEVICES
    for t, (steps, core) in enumerate(OFFSETS):
        source = offset_index(me, HEAD_DEVICES // 2 - steps, core)
        own_ref[pl.ds(pl.multiple_of(source * mine, mine), mine), :] = parts[t][...]
    for b in range(LEVELS):
        for s in range(SEND):
            out_refs[b][s * BLK : (s + 1) * BLK, :] = own_ref[rows_of(sends_ref[b, s]), :]
    copy.wait()


def pick(sends, parts, grad):
    return pl.pallas_call(
        pick_kernel,
        out_shape=[pltpu.VMEM((OWN, 2 * WIDE), BF16), pltpu.VMEM((OWN, WIDE), BF16)]
        + [pltpu.VMEM((PART, 2 * WIDE), BF16)] * LEVELS,
        in_specs=[SM, HB] + [VM] * HEAD_DEVICES,
        out_specs=[VM] * (2 + LEVELS),
        scratch_shapes=[pltpu.SemaphoreType.DMA],
        compiler_params=limits(8),
        cost_estimate=pl.CostEstimate(flops=0, bytes_accessed=4 * 2**20, transcendentals=0),
        name="pick_boundary",
    )(sends, pltpu.with_memory_space_constraint(grad, pltpu.HBM), *parts)


def pixel_grads(i, live, kv, q_ref, g_ref, att_ref, qg_ref, outs):
    at = rows_of(i)
    q = q_ref[at, :] * jnp.array(HD**-0.5, BF16)
    g = g_ref[at, :]
    low = lax.broadcasted_iota(jnp.int32, (BLK, WIDE), 1) < HD
    z = jnp.zeros((BLK, WIDE), BF16)
    both = jnp.concatenate(
        [
            jnp.concatenate([jnp.where(low, q, z), z], 1),
            jnp.concatenate([jnp.where(low, z, q), z], 1),
            jnp.concatenate([z, jnp.where(low, g, z)], 1),
            jnp.concatenate([z, jnp.where(low, z, g)], 1),
        ],
        0,
    )
    sd = lax.dot_general(kv, both, (((1,), (1,)), ((), ())), preferred_element_type=F32)
    s = [sd[j * BLK : (j + 1) * BLK, :WIDE] for j in range(NNB)]
    d = [sd[j * BLK : (j + 1) * BLK, WIDE:] for j in range(NNB)]
    s[-1] = jnp.where(live, s[-1], FILL)
    peak = functools.reduce(jnp.maximum, s)
    peak = jnp.max(peak, 0, keepdims=True)
    p = [jnp.exp(x - peak) for x in s]
    total = jnp.sum(sum(p[1:], p[0]), 0, keepdims=True)
    dot = [x * y for x, y in zip(p, d)]
    inv = 1.0 / total
    dot = jnp.sum(sum(dot[1:], dot[0]), 0, keepdims=True) * inv
    weights = [x * inv for x in p]
    rounded = jnp.concatenate([x.astype(BF16) for x in weights], 0)
    grads = jnp.concatenate([(x * (y - dot)).astype(BF16) for x, y in zip(weights, d)], 0)
    terms = lax.dot_general(
        jnp.concatenate([grads, rounded], 1), both, (((1,), (0,)), ((), ())), preferred_element_type=F32
    )
    down = (((0,), (0,)), ((), ()))
    qg = lax.dot_general(grads, kv[:, :WIDE], down, preferred_element_type=F32)
    att = lax.dot_general(rounded, kv[:, WIDE:], down, preferred_element_type=F32)
    att_ref[at, :] = jnp.where(low, att[:BLK], att[BLK:]).astype(BF16)
    qg_ref[at, :] = (jnp.where(low, qg[:BLK], qg[BLK:]) * HD**-0.5).astype(BF16)
    for copy in outs(i):
        copy.start()
    return [terms[j * BLK : (j + 1) * BLK] for j in range(NNB)]


def row_copies(at, staged, outs, sems):
    return [
        pltpu.make_async_copy(x.at[rows_of(at), :], y.at[rows_of(at), :], sems.at[n, at])
        for n, (x, y) in enumerate(zip(staged, outs))
    ]


def inner_kernel(unroll, rows_ref, counts_ref, q_ref, g_ref, own_ref, att_ref, qg_ref, acc_ref, *refs):
    list_ref, staged, sems = refs[0], refs[1:3], refs[3]
    outs = lambda i: row_copies(i, staged, (att_ref, qg_ref), sems)
    steps = NBLK - LEVELS * SEND
    acc_ref[...] = jnp.zeros_like(acc_ref)

    def note(i, count):
        list_ref[count] = i
        return count + (rows_ref[i, 1] < NBLK).astype(jnp.int32)

    lax.fori_loop(0, NBLK, note, jnp.int32(0))

    def step(t, carry):
        for u in range(unroll):
            i = list_ref[t * unroll + u]
            at = [rows_of(rows_ref[i, j]) for j in range(NNB)]
            kv = jnp.concatenate([own_ref[a, :] for a in at], 0)
            terms = pixel_grads(i, counts_ref[i] > NNB - 1, kv, q_ref, g_ref, *staged, outs)
            for j in range(NNB):
                acc_ref[at[j], :] += terms[j]
        return carry

    lax.fori_loop(0, steps // unroll, step, 0)

    def settle(t, carry):
        for copy in outs(list_ref[t]):
            copy.wait()
        return carry

    lax.fori_loop(0, steps, settle, 0)


def inner(rows, counts, q, g, own):
    return pl.pallas_call(
        functools.partial(inner_kernel, 2),
        out_shape=[
            pltpu.HBM((OWN, WIDE), BF16),
            pltpu.HBM((OWN, WIDE), BF16),
            pltpu.VMEM((OWN, 2 * WIDE), F32),
        ],
        in_specs=[SM, SM] + [VM] * 3,
        out_specs=[HB, HB, VM],
        scratch_shapes=[pltpu.SMEM((NBLK + 1,), jnp.int32)]
        + [pltpu.VMEM((OWN, WIDE), BF16)] * 2
        + [pltpu.SemaphoreType.DMA((2, NBLK))],
        compiler_params=limits(16),
        cost_estimate=pl.CostEstimate(flops=4 * 10**9, bytes_accessed=8 * 2**20, transcendentals=10**6),
        name="attend_inner",
    )(rows, counts, q, g, own)


def outer_kernel(unroll, sends_ref, rows_ref, counts_ref, q_ref, g_ref, own_ref, *refs):
    recv_refs, refs = refs[:LEVELS], refs[LEVELS + 3 :]
    att_ref, qg_ref, acc_ref = refs[:3]
    back_refs, refs = refs[3 : 3 + LEVELS], refs[3 + LEVELS :]
    far_ref, back_ref, staged, sems, back_sems = refs[0], refs[1], refs[2:4], refs[4], refs[5]
    outs = lambda i: row_copies(i, staged, (att_ref, qg_ref), sems)
    backs = [
        pltpu.make_async_copy(back_ref.at[b * PART : (b + 1) * PART, :], back_refs[b], back_sems.at[b])
        for b in range(LEVELS)
    ]
    for b in range(LEVELS):
        far_ref[b * PART : (b + 1) * PART, :] = recv_refs[b][...]

    def step(t, carry):
        for u in range(unroll):
            e = t * unroll + u
            i = sends_ref[e // SEND, e % SEND]
            at = [rows_of(rows_ref[i, j]) if j != 1 else None for j in range(NNB)]
            far = rows_of(e)
            kv = jnp.concatenate([own_ref[a, :] if a is not None else far_ref[far, :] for a in at], 0)
            terms = pixel_grads(i, counts_ref[i] > NNB - 1, kv, q_ref, g_ref, *staged, outs)
            for j in range(NNB):
                if j == 1:
                    back_ref[far, :] = terms[j].astype(BF16)
                else:
                    acc_ref[at[j], :] += terms[j]
        for b in range(LEVELS):
            pl.when(t == (b + 1) * SEND // unroll - 1)(backs[b].start)
        return carry

    lax.fori_loop(0, LEVELS * SEND // unroll, step, 0)

    def settle(e, carry):
        for copy in outs(sends_ref[e // SEND, e % SEND]):
            copy.wait()
        return carry

    lax.fori_loop(0, LEVELS * SEND, settle, 0)
    for copy in backs:
        copy.wait()


def outer(sends, rows, counts, q, g, own, recv, done):
    far = (LEVELS * PART, 2 * WIDE)
    return pl.pallas_call(
        functools.partial(outer_kernel, 2),
        out_shape=[
            pltpu.HBM((OWN, WIDE), BF16),
            pltpu.HBM((OWN, WIDE), BF16),
            pltpu.VMEM((OWN, 2 * WIDE), F32),
        ]
        + [pltpu.HBM((PART, 2 * WIDE), BF16)] * LEVELS,
        in_specs=[SM] * 3 + [VM] * (3 + LEVELS) + [HB, HB, VM],
        out_specs=[HB, HB, VM] + [HB] * LEVELS,
        scratch_shapes=[pltpu.VMEM(far, BF16), pltpu.VMEM(far, BF16)]
        + [pltpu.VMEM((OWN, WIDE), BF16)] * 2
        + [pltpu.SemaphoreType.DMA((2, NBLK)), pltpu.SemaphoreType.DMA((LEVELS,))],
        input_output_aliases={6 + LEVELS + n: n for n in range(3)},
        compiler_params=limits(16),
        cost_estimate=pl.CostEstimate(flops=8 * 10**9, bytes_accessed=8 * 2**20, transcendentals=2 * 10**6),
        name="attend_outer",
    )(sends, rows, counts, q, g, own, *recv, *done)


def join_kernel(sends_ref, acc_ref, *refs):
    arrived_refs = refs[:LEVELS]
    key_ref, value_ref = refs[LEVELS : LEVELS + 2]
    key_ref[...] = acc_ref[:, :WIDE].astype(BF16)
    value_ref[...] = acc_ref[:, WIDE:].astype(BF16)
    for b in range(LEVELS):
        for s in range(SEND):
            at = rows_of(sends_ref[b, s])
            both = acc_ref[at, :] + arrived_refs[b][s * BLK : (s + 1) * BLK, :].astype(F32)
            key_ref[at, :] = both[:, :WIDE].astype(BF16)
            value_ref[at, :] = both[:, WIDE:].astype(BF16)


def join(sends, acc, arrived):
    return pl.pallas_call(
        join_kernel,
        out_shape=[jax.ShapeDtypeStruct((OWN, WIDE), BF16)] * 2,
        in_specs=[SM] + [VM] * (1 + LEVELS),
        out_specs=[VM] * 2,
        compiler_params=limits(10),
        cost_estimate=pl.CostEstimate(flops=10**6, bytes_accessed=4 * 2**20, transcendentals=0),
        name="join_gradients",
    )(sends, acc, *arrived)


def body(query_rows, key_rows, value_rows, out_grad, boundary_send_blocks, neighbours, live_count):
    heads = lax.axis_size("head")
    mine = query_rows.shape[0]
    my_range = lax.axis_index("pix")
    sends = lax.dynamic_index_in_dim(boundary_send_blocks, my_range, 0, keepdims=False)
    rows = lax.dynamic_slice_in_dim(neighbours, my_range * NBLK, NBLK, 0)
    counts = lax.dynamic_slice_in_dim(live_count, my_range * NBLK, NBLK, 0)

    parts = split(key_rows, value_rows)
    parts = [shifted(x, *o) if o != (0, 0) else x for x, o in zip(parts, OFFSETS)]
    q = query_rows.reshape(mine, heads, WIDE).transpose(1, 0, 2)
    q, parts[0] = lax.optimization_barrier((q, parts[0]))
    q = lax.all_to_all(q, "head", 0, 0, tiled=True).reshape(OWN, WIDE)
    own, grad, *outgoing = pick(sends, parts, out_grad)
    recv = [swapped(outgoing[b], b) for b in range(LEVELS)]
    done = inner(rows, counts, q, grad, own)
    attended, query_grad, acc, *back = outer(sends, rows, counts, q, grad, own, recv, done)
    arrived = [swapped(back[b], b) for b in range(LEVELS)]
    attended = lax.all_to_all(attended.reshape(heads, mine, WIDE), "head", 0, 0, tiled=True)
    attended = attended.transpose(1, 0, 2).reshape(mine, heads * WIDE)
    key_grad, value_grad = join(sends, acc, arrived)
    return attended, query_grad, key_grad, value_grad


def solution(mesh):
    rows = P(("pix", "head"), None)
    split = P("pix", "head")
    return jax.shard_map(
        body,
        mesh=mesh,
        in_specs=(rows, rows, rows, split, P(), P(), P()),
        out_specs=(rows, split, split, split),
        check_vma=False,
    )
```

```python
import functools
import jax
import jax.numpy as jnp
from jax import lax
from jax.experimental import pallas as pl
from jax.experimental.pallas import tpu as pltpu
from jax.sharding import PartitionSpec as P

HD = 64
BLK = 64
NNB = 9
NBLK = 32
LEVELS = 5
SEND = 4
WIDE = 2 * HD
OWN = NBLK * BLK
PART = SEND * BLK
FILL = -1e30
CHUNKS = 8
HEAD_DEVICES = 8
OFFSETS = ((1, 0), (3, 0), (1, 1), (3, 1), (2, 0), (2, 1), (0, 1), (0, 0))
F32 = jnp.float32
BF16 = jnp.bfloat16

VM = pl.BlockSpec(memory_space=pltpu.VMEM)
SM = pl.BlockSpec(memory_space=pltpu.SMEM)
HB = pl.BlockSpec(memory_space=pltpu.HBM)


def swapped(block, bit):
    count = lax.axis_size("pix")
    route = [(low, low ^ (1 << bit)) for low in range(count)]
    return lax.ppermute(block, "pix", route)


def rows_of(start):
    return pl.ds(pl.multiple_of(start * BLK, BLK), BLK)


def offset_index(index, steps, core):
    chips = HEAD_DEVICES // 2
    return (index // 2 + steps) % chips * 2 + (index % 2 + core) % 2


def shifted(block, steps, core):
    route = [(i, offset_index(i, steps, core)) for i in range(HEAD_DEVICES)]
    return lax.ppermute(block, "head", route)


def limits(megabytes):
    return pltpu.CompilerParams(vmem_limit_bytes=megabytes * 2**20)


def split_kernel(key_ref, value_ref, *refs):
    parts, sems = refs[:-1], refs[-1]
    me = lax.axis_index("head")
    copies = []
    for t, (steps, core) in enumerate(OFFSETS):
        column = pl.ds(pl.multiple_of(offset_index(me, steps, core) * WIDE, WIDE), WIDE)
        for n, ref in enumerate((key_ref, value_ref)):
            copies.append(
                pltpu.make_async_copy(
                    ref.at[:, column], parts[t].at[:, n * WIDE : (n + 1) * WIDE], sems.at[2 * t + n]
                )
            )
    for copy in copies:
        copy.start()
    for copy in copies:
        copy.wait()


def split(keys, values):
    mine = keys.shape[0]
    return pl.pallas_call(
        split_kernel,
        out_shape=[pltpu.VMEM((mine, 2 * WIDE), BF16)] * HEAD_DEVICES,
        in_specs=[HB] * 2,
        out_specs=[VM] * HEAD_DEVICES,
        scratch_shapes=[pltpu.SemaphoreType.DMA((2 * HEAD_DEVICES,))],
        compiler_params=limits(4),
        cost_estimate=pl.CostEstimate(flops=0, bytes_accessed=2 * 2**20, transcendentals=0),
        name="split_keys_values",
    )(pltpu.with_memory_space_constraint(keys, pltpu.HBM), pltpu.with_memory_space_constraint(values, pltpu.HBM))


def pick_kernel(sends_ref, *refs):
    parts, refs = refs[:HEAD_DEVICES], refs[HEAD_DEVICES:]
    own_ref, out_refs, held_ref, sems = refs[0], refs[1 : 1 + LEVELS], refs[-2], refs[-1]
    me = lax.axis_index("head")
    mine = OWN // HEAD_DEVICES
    copies = []
    for t, (steps, core) in enumerate(OFFSETS):
        source = offset_index(me, HEAD_DEVICES // 2 - steps, core)
        at = pl.ds(pl.multiple_of(source * mine, mine), mine)
        copies.append(pltpu.make_async_copy(parts[t], own_ref.at[at, :], sems.at[t]))
        copies[-1].start()
        held_ref[at, :] = parts[t][...]
    for b in range(LEVELS):
        for s in range(SEND):
            out_refs[b][s * BLK : (s + 1) * BLK, :] = held_ref[rows_of(sends_ref[b, s]), :]
    for copy in copies:
        copy.wait()


def pick(sends, parts):
    return pl.pallas_call(
        pick_kernel,
        out_shape=[pltpu.HBM((OWN, 2 * WIDE), BF16)] + [pltpu.VMEM((PART, 2 * WIDE), BF16)] * LEVELS,
        in_specs=[SM] + [VM] * HEAD_DEVICES,
        out_specs=[HB] + [VM] * LEVELS,
        scratch_shapes=[pltpu.VMEM((OWN, 2 * WIDE), BF16), pltpu.SemaphoreType.DMA((HEAD_DEVICES,))],
        compiler_params=limits(8),
        cost_estimate=pl.CostEstimate(flops=0, bytes_accessed=4 * 2**20, transcendentals=0),
        name="pick_boundary",
    )(sends, *parts)


def pixel_grads(i, live, kv, q_ref, g_ref, att_ref, qg_ref, outs):
    at = rows_of(i)
    q = q_ref[at, :] * jnp.array(HD**-0.5, BF16)
    g = g_ref[at, :]
    low = lax.broadcasted_iota(jnp.int32, (BLK, WIDE), 1) < HD
    z = jnp.zeros((BLK, WIDE), BF16)
    both = jnp.concatenate(
        [
            jnp.concatenate([jnp.where(low, q, z), z], 1),
            jnp.concatenate([jnp.where(low, z, q), z], 1),
            jnp.concatenate([z, jnp.where(low, g, z)], 1),
            jnp.concatenate([z, jnp.where(low, z, g)], 1),
        ],
        0,
    )
    sd = lax.dot_general(kv, both, (((1,), (1,)), ((), ())), preferred_element_type=F32)
    s = [sd[j * BLK : (j + 1) * BLK, :WIDE] for j in range(NNB)]
    d = [sd[j * BLK : (j + 1) * BLK, WIDE:] for j in range(NNB)]
    s[-1] = jnp.where(live, s[-1], FILL)
    peak = functools.reduce(jnp.maximum, s)
    peak = jnp.max(peak, 0, keepdims=True)
    p = [jnp.exp(x - peak) for x in s]
    total = jnp.sum(sum(p[1:], p[0]), 0, keepdims=True)
    dot = [x * y for x, y in zip(p, d)]
    inv = 1.0 / total
    dot = jnp.sum(sum(dot[1:], dot[0]), 0, keepdims=True) * inv
    weights = [x * inv for x in p]
    rounded = jnp.concatenate([x.astype(BF16) for x in weights], 0)
    grads = jnp.concatenate([(x * (y - dot)).astype(BF16) for x, y in zip(weights, d)], 0)
    terms = lax.dot_general(
        jnp.concatenate([grads, rounded], 1), both, (((1,), (0,)), ((), ())), preferred_element_type=F32
    )
    down = (((0,), (0,)), ((), ()))
    qg = lax.dot_general(grads, kv[:, :WIDE], down, preferred_element_type=F32)
    att = lax.dot_general(rounded, kv[:, WIDE:], down, preferred_element_type=F32)
    att_ref[at, :] = jnp.where(low, att[:BLK], att[BLK:]).astype(BF16)
    qg_ref[at, :] = (jnp.where(low, qg[:BLK], qg[BLK:]) * HD**-0.5).astype(BF16)
    for copy in outs(i):
        copy.start()
    return [terms[j * BLK : (j + 1) * BLK] for j in range(NNB)]


def row_copies(at, staged, outs, sems):
    return [
        pltpu.make_async_copy(x.at[rows_of(at), :], y.at[rows_of(at), :], sems.at[n, at])
        for n, (x, y) in enumerate(zip(staged, outs))
    ]


def inner_kernel(unroll, rows_ref, counts_ref, q_ref, far_g_ref, far_own_ref, *refs):
    att_ref, qg_ref, acc_ref, own_ref, g_ref, list_ref = refs[:6]
    staged, sems, in_sems = refs[6:8], refs[8], refs[9]
    loads = []
    for n, (x, y) in enumerate(((far_own_ref, own_ref), (far_g_ref, g_ref))):
        for c in range(CHUNKS):
            part = pl.ds(c * (OWN // CHUNKS), OWN // CHUNKS)
            loads.append(pltpu.make_async_copy(x.at[part, :], y.at[part, :], in_sems.at[n, c]))
            loads[-1].start()
    outs = lambda i: row_copies(i, staged, (att_ref, qg_ref), sems)
    steps = NBLK - LEVELS * SEND
    acc_ref[...] = jnp.zeros_like(acc_ref)

    def note(i, count):
        list_ref[count] = i
        return count + (rows_ref[i, 1] < NBLK).astype(jnp.int32)

    lax.fori_loop(0, NBLK, note, jnp.int32(0))
    for load in loads:
        load.wait()

    def step(t, carry):
        for u in range(unroll):
            i = list_ref[t * unroll + u]
            at = [rows_of(rows_ref[i, j]) for j in range(NNB)]
            kv = jnp.concatenate([own_ref[a, :] for a in at], 0)
            terms = pixel_grads(i, counts_ref[i] > NNB - 1, kv, q_ref, g_ref, *staged, outs)
            for j in range(NNB):
                acc_ref[at[j], :] += terms[j]
        return carry

    lax.fori_loop(0, steps // unroll, step, 0)

    def settle(t, carry):
        for copy in outs(list_ref[t]):
            copy.wait()
        return carry

    lax.fori_loop(0, steps, settle, 0)


def inner(rows, counts, q, g, own):
    return pl.pallas_call(
        functools.partial(inner_kernel, 2),
        out_shape=[
            pltpu.HBM((OWN, WIDE), BF16),
            pltpu.HBM((OWN, WIDE), BF16),
            pltpu.VMEM((OWN, 2 * WIDE), F32),
            pltpu.VMEM((OWN, 2 * WIDE), BF16),
            pltpu.VMEM((OWN, WIDE), BF16),
        ],
        in_specs=[SM, SM, VM, HB, HB],
        out_specs=[HB, HB, VM, VM, VM],
        scratch_shapes=[pltpu.SMEM((NBLK + 1,), jnp.int32)]
        + [pltpu.VMEM((OWN, WIDE), BF16)] * 2
        + [pltpu.SemaphoreType.DMA((2, NBLK)), pltpu.SemaphoreType.DMA((2, CHUNKS))],
        compiler_params=limits(16),
        cost_estimate=pl.CostEstimate(flops=4 * 10**9, bytes_accessed=8 * 2**20, transcendentals=10**6),
        name="attend_inner",
    )(rows, counts, q, *(pltpu.with_memory_space_constraint(x, pltpu.HBM) for x in (g, own)))


def outer_kernel(unroll, sends_ref, rows_ref, counts_ref, q_ref, g_ref, own_ref, *refs):
    recv_refs, refs = refs[:LEVELS], refs[LEVELS + 3 :]
    att_ref, qg_ref, acc_ref = refs[:3]
    back_refs, refs = refs[3 : 3 + LEVELS], refs[3 + LEVELS :]
    far_ref, back_ref, staged, sems, back_sems = refs[0], refs[1], refs[2:4], refs[4], refs[5]
    outs = lambda i: row_copies(i, staged, (att_ref, qg_ref), sems)
    backs = [
        pltpu.make_async_copy(back_ref.at[b * PART : (b + 1) * PART, :], back_refs[b], back_sems.at[b])
        for b in range(LEVELS)
    ]
    for b in range(LEVELS):
        far_ref[b * PART : (b + 1) * PART, :] = recv_refs[b][...]

    def step(t, carry):
        for u in range(unroll):
            e = t * unroll + u
            i = sends_ref[e // SEND, e % SEND]
            at = [rows_of(rows_ref[i, j]) if j != 1 else None for j in range(NNB)]
            far = rows_of(e)
            kv = jnp.concatenate([own_ref[a, :] if a is not None else far_ref[far, :] for a in at], 0)
            terms = pixel_grads(i, counts_ref[i] > NNB - 1, kv, q_ref, g_ref, *staged, outs)
            for j in range(NNB):
                if j == 1:
                    back_ref[far, :] = terms[j].astype(BF16)
                else:
                    acc_ref[at[j], :] += terms[j]
        for b in range(LEVELS):
            pl.when(t == (b + 1) * SEND // unroll - 1)(backs[b].start)
        return carry

    lax.fori_loop(0, LEVELS * SEND // unroll, step, 0)

    def settle(e, carry):
        for copy in outs(sends_ref[e // SEND, e % SEND]):
            copy.wait()
        return carry

    lax.fori_loop(0, LEVELS * SEND, settle, 0)
    for copy in backs:
        copy.wait()


def outer(sends, rows, counts, q, g, own, recv, done):
    far = (LEVELS * PART, 2 * WIDE)
    return pl.pallas_call(
        functools.partial(outer_kernel, 2),
        out_shape=[
            pltpu.HBM((OWN, WIDE), BF16),
            pltpu.HBM((OWN, WIDE), BF16),
            pltpu.VMEM((OWN, 2 * WIDE), F32),
        ]
        + [pltpu.HBM((PART, 2 * WIDE), BF16)] * LEVELS,
        in_specs=[SM] * 3 + [VM] * (3 + LEVELS) + [HB, HB, VM],
        out_specs=[HB, HB, VM] + [HB] * LEVELS,
        scratch_shapes=[pltpu.VMEM(far, BF16), pltpu.VMEM(far, BF16)]
        + [pltpu.VMEM((OWN, WIDE), BF16)] * 2
        + [pltpu.SemaphoreType.DMA((2, NBLK)), pltpu.SemaphoreType.DMA((LEVELS,))],
        input_output_aliases={6 + LEVELS + n: n for n in range(3)},
        compiler_params=limits(16),
        cost_estimate=pl.CostEstimate(flops=8 * 10**9, bytes_accessed=8 * 2**20, transcendentals=2 * 10**6),
        name="attend_outer",
    )(sends, rows, counts, q, g, own, *recv, *done)


def join_kernel(sends_ref, acc_ref, *refs):
    arrived_refs = refs[:LEVELS]
    key_ref, value_ref = refs[LEVELS : LEVELS + 2]
    key_ref[...] = acc_ref[:, :WIDE].astype(BF16)
    value_ref[...] = acc_ref[:, WIDE:].astype(BF16)
    for b in range(LEVELS):
        for s in range(SEND):
            at = rows_of(sends_ref[b, s])
            both = acc_ref[at, :] + arrived_refs[b][s * BLK : (s + 1) * BLK, :].astype(F32)
            key_ref[at, :] = both[:, :WIDE].astype(BF16)
            value_ref[at, :] = both[:, WIDE:].astype(BF16)


def join(sends, acc, arrived):
    return pl.pallas_call(
        join_kernel,
        out_shape=[jax.ShapeDtypeStruct((OWN, WIDE), BF16)] * 2,
        in_specs=[SM] + [VM] * (1 + LEVELS),
        out_specs=[VM] * 2,
        compiler_params=limits(10),
        cost_estimate=pl.CostEstimate(flops=10**6, bytes_accessed=4 * 2**20, transcendentals=0),
        name="join_gradients",
    )(sends, acc, *arrived)


def body(query_rows, key_rows, value_rows, out_grad, boundary_send_blocks, neighbours, live_count):
    heads = lax.axis_size("head")
    mine = query_rows.shape[0]
    my_range = lax.axis_index("pix")
    sends = lax.dynamic_index_in_dim(boundary_send_blocks, my_range, 0, keepdims=False)
    rows = lax.dynamic_slice_in_dim(neighbours, my_range * NBLK, NBLK, 0)
    counts = lax.dynamic_slice_in_dim(live_count, my_range * NBLK, NBLK, 0)

    parts = split(key_rows, value_rows)
    parts = [shifted(x, *o) if o != (0, 0) else x for x, o in zip(parts, OFFSETS)]
    q = query_rows.reshape(mine, heads, WIDE).transpose(1, 0, 2)
    own, *outgoing = pick(sends, parts)
    q, own = lax.optimization_barrier((q, own))
    q = lax.all_to_all(q, "head", 0, 0, tiled=True).reshape(OWN, WIDE)
    recv = [swapped(outgoing[b], b) for b in range(LEVELS)]
    *done, own, grad = inner(rows, counts, q, out_grad, own)
    attended, query_grad, acc, *back = outer(sends, rows, counts, q, grad, own, recv, done)
    arrived = [swapped(back[b], b) for b in range(LEVELS)]
    attended = lax.all_to_all(attended.reshape(heads, mine, WIDE), "head", 0, 0, tiled=True)
    attended = attended.transpose(1, 0, 2).reshape(mine, heads * WIDE)
    key_grad, value_grad = join(sends, acc, arrived)
    return attended, query_grad, key_grad, value_grad


def solution(mesh):
    rows = P(("pix", "head"), None)
    split = P("pix", "head")
    return jax.shard_map(
        body,
        mesh=mesh,
        in_specs=(rows, rows, rows, split, P(), P(), P()),
        out_specs=(rows, split, split, split),
        check_vma=False,
    )
```

```python
import functools
import jax
import jax.numpy as jnp
from jax import lax
from jax.experimental import pallas as pl
from jax.experimental.pallas import tpu as pltpu
from jax.sharding import PartitionSpec as P

HD = 64
BLK = 64
NNB = 9
NBLK = 32
LEVELS = 5
SEND = 4
WIDE = 2 * HD
OWN = NBLK * BLK
PART = SEND * BLK
FILL = -1e30
CHUNKS = 8
HEAD_DEVICES = 8
OFFSETS = ((1, 0), (3, 0), (1, 1), (3, 1), (2, 0), (2, 1), (0, 1), (0, 0))
F32 = jnp.float32
BF16 = jnp.bfloat16

VM = pl.BlockSpec(memory_space=pltpu.VMEM)
SM = pl.BlockSpec(memory_space=pltpu.SMEM)
HB = pl.BlockSpec(memory_space=pltpu.HBM)


def swapped(block, bit):
    count = lax.axis_size("pix")
    route = [(low, low ^ (1 << bit)) for low in range(count)]
    return lax.ppermute(block, "pix", route)


def rows_of(start):
    return pl.ds(pl.multiple_of(start * BLK, BLK), BLK)


def offset_index(index, steps, core):
    chips = HEAD_DEVICES // 2
    return (index // 2 + steps) % chips * 2 + (index % 2 + core) % 2


def shifted(block, steps, core):
    route = [(i, offset_index(i, steps, core)) for i in range(HEAD_DEVICES)]
    return lax.ppermute(block, "head", route)


def limits(megabytes):
    return pltpu.CompilerParams(vmem_limit_bytes=megabytes * 2**20)


def split_kernel(key_ref, value_ref, *refs):
    parts, sems = refs[:-1], refs[-1]
    me = lax.axis_index("head")
    copies = []
    for t, (steps, core) in enumerate(OFFSETS):
        column = pl.ds(pl.multiple_of(offset_index(me, steps, core) * WIDE, WIDE), WIDE)
        for n, ref in enumerate((key_ref, value_ref)):
            copies.append(
                pltpu.make_async_copy(
                    ref.at[:, column], parts[t].at[:, n * WIDE : (n + 1) * WIDE], sems.at[2 * t + n]
                )
            )
    for copy in copies:
        copy.start()
    for copy in copies:
        copy.wait()


def split(keys, values):
    mine = keys.shape[0]
    return pl.pallas_call(
        split_kernel,
        out_shape=[pltpu.VMEM((mine, 2 * WIDE), BF16)] * HEAD_DEVICES,
        in_specs=[HB] * 2,
        out_specs=[VM] * HEAD_DEVICES,
        scratch_shapes=[pltpu.SemaphoreType.DMA((2 * HEAD_DEVICES,))],
        compiler_params=limits(4),
        cost_estimate=pl.CostEstimate(flops=0, bytes_accessed=2 * 2**20, transcendentals=0),
        name="split_keys_values",
    )(pltpu.with_memory_space_constraint(keys, pltpu.HBM), pltpu.with_memory_space_constraint(values, pltpu.HBM))


def pick_kernel(sends_ref, *refs):
    parts, refs = refs[:HEAD_DEVICES], refs[HEAD_DEVICES:]
    own_ref, out_refs, held_ref, sems = refs[0], refs[1 : 1 + LEVELS], refs[-2], refs[-1]
    me = lax.axis_index("head")
    mine = OWN // HEAD_DEVICES
    copies = []
    for t, (steps, core) in enumerate(OFFSETS):
        source = offset_index(me, HEAD_DEVICES // 2 - steps, core)
        at = pl.ds(pl.multiple_of(source * mine, mine), mine)
        copies.append(pltpu.make_async_copy(parts[t], own_ref.at[at, :], sems.at[t]))
        copies[-1].start()
        held_ref[at, :] = parts[t][...]
    for b in range(LEVELS):
        for s in range(SEND):
            out_refs[b][s * BLK : (s + 1) * BLK, :] = held_ref[rows_of(sends_ref[b, s]), :]
    for copy in copies:
        copy.wait()


def pick(sends, parts):
    return pl.pallas_call(
        pick_kernel,
        out_shape=[pltpu.HBM((OWN, 2 * WIDE), BF16)] + [pltpu.VMEM((PART, 2 * WIDE), BF16)] * LEVELS,
        in_specs=[SM] + [VM] * HEAD_DEVICES,
        out_specs=[HB] + [VM] * LEVELS,
        scratch_shapes=[pltpu.VMEM((OWN, 2 * WIDE), BF16), pltpu.SemaphoreType.DMA((HEAD_DEVICES,))],
        compiler_params=limits(8),
        cost_estimate=pl.CostEstimate(flops=0, bytes_accessed=4 * 2**20, transcendentals=0),
        name="pick_boundary",
    )(sends, *parts)


def staged_block(i, live, at, far, q_ref, g_ref, own_ref, acc_ref, staged, outs):
    rows = rows_of(i)
    q = q_ref[rows, :] * jnp.array(HD**-0.5, BF16)
    g = g_ref[rows, :]
    low = lax.broadcasted_iota(jnp.int32, (BLK, WIDE), 1) < HD
    z = jnp.zeros((BLK, WIDE), BF16)
    q = jnp.concatenate([jnp.where(low, q, z), jnp.where(low, z, q)], 0)
    g = jnp.concatenate([jnp.where(low, g, z), jnp.where(low, z, g)], 0)
    blocks = [own_ref[a, :] if a is not None else far[0][...] for a in at]
    kv = jnp.concatenate(blocks, 0)
    product = functools.partial(lax.dot_general, preferred_element_type=F32)
    across, plain, down = (((1,), (1,)), ((), ())), (((1,), (0,)), ((), ())), (((0,), (0,)), ((), ()))
    s = product(kv[:, :WIDE], q, across)
    d = product(kv[:, WIDE:], g, across)
    yield
    s = [s[j * BLK : (j + 1) * BLK] for j in range(NNB)]
    d = [d[j * BLK : (j + 1) * BLK] for j in range(NNB)]
    s[-1] = jnp.where(live, s[-1], FILL)
    peak = jnp.max(functools.reduce(jnp.maximum, s), 0, keepdims=True)
    p = [jnp.exp(x - peak) for x in s]
    total = jnp.sum(sum(p[1:], p[0]), 0, keepdims=True)
    dot = [x * y for x, y in zip(p, d)]
    inv = 1.0 / total
    dot = jnp.sum(sum(dot[1:], dot[0]), 0, keepdims=True) * inv
    weights = [x * inv for x in p]
    rounded = jnp.concatenate([x.astype(BF16) for x in weights], 0)
    grads = jnp.concatenate([(x * (y - dot)).astype(BF16) for x, y in zip(weights, d)], 0)
    yield
    terms = jnp.concatenate([product(grads, q, plain), product(rounded, g, plain)], 1)
    for j in range(NNB):
        term = terms[j * BLK : (j + 1) * BLK]
        if at[j] is None:
            far[1][...] = term.astype(BF16)
        else:
            acc_ref[at[j], :] += term
    yield
    results = product(jnp.concatenate([grads, rounded], 1), kv, down)
    qg, att = results[:WIDE, :WIDE], results[WIDE:, WIDE:]
    staged[0][rows, :] = jnp.where(low, att[:BLK], att[BLK:]).astype(BF16)
    staged[1][rows, :] = (jnp.where(low, qg[:BLK], qg[BLK:]) * HD**-0.5).astype(BF16)
    for copy in outs(i):
        copy.start()
    yield


def run_staged(blocks):
    stages = 4
    for t in range(len(blocks) + stages - 1):
        for k in reversed(range(stages)):
            if 0 <= t - k < len(blocks):
                next(blocks[t - k])


def row_copies(at, staged, outs, sems):
    return [
        pltpu.make_async_copy(x.at[rows_of(at), :], y.at[rows_of(at), :], sems.at[n, at])
        for n, (x, y) in enumerate(zip(staged, outs))
    ]


def inner_kernel(unroll, rows_ref, counts_ref, q_ref, far_g_ref, far_own_ref, *refs):
    att_ref, qg_ref, acc_ref, own_ref, g_ref, list_ref = refs[:6]
    staged, sems, in_sems = refs[6:8], refs[8], refs[9]
    loads = []
    for n, (x, y) in enumerate(((far_own_ref, own_ref), (far_g_ref, g_ref))):
        for c in range(CHUNKS):
            part = pl.ds(c * (OWN // CHUNKS), OWN // CHUNKS)
            loads.append(pltpu.make_async_copy(x.at[part, :], y.at[part, :], in_sems.at[n, c]))
            loads[-1].start()
    outs = lambda i: row_copies(i, staged, (att_ref, qg_ref), sems)
    steps = NBLK - LEVELS * SEND
    acc_ref[...] = jnp.zeros_like(acc_ref)

    def note(i, count):
        list_ref[count] = i
        return count + (rows_ref[i, 1] < NBLK).astype(jnp.int32)

    lax.fori_loop(0, NBLK, note, jnp.int32(0))
    for load in loads:
        load.wait()

    def step(t, carry):
        blocks = []
        for u in range(unroll):
            i = list_ref[t * unroll + u]
            at = [rows_of(rows_ref[i, j]) for j in range(NNB)]
            live = counts_ref[i] > NNB - 1
            blocks.append(staged_block(i, live, at, None, q_ref, g_ref, own_ref, acc_ref, staged, outs))
        run_staged(blocks)
        return carry

    lax.fori_loop(0, steps // unroll, step, 0)

    def settle(t, carry):
        for copy in outs(list_ref[t]):
            copy.wait()
        return carry

    lax.fori_loop(0, steps, settle, 0)


def inner(rows, counts, q, g, own):
    return pl.pallas_call(
        functools.partial(inner_kernel, 12),
        out_shape=[
            pltpu.HBM((OWN, WIDE), BF16),
            pltpu.HBM((OWN, WIDE), BF16),
            pltpu.VMEM((OWN, 2 * WIDE), F32),
            pltpu.VMEM((OWN, 2 * WIDE), BF16),
            pltpu.VMEM((OWN, WIDE), BF16),
        ],
        in_specs=[SM, SM, VM, HB, HB],
        out_specs=[HB, HB, VM, VM, VM],
        scratch_shapes=[pltpu.SMEM((NBLK + 1,), jnp.int32)]
        + [pltpu.VMEM((OWN, WIDE), BF16)] * 2
        + [pltpu.SemaphoreType.DMA((2, NBLK)), pltpu.SemaphoreType.DMA((2, CHUNKS))],
        compiler_params=limits(16),
        cost_estimate=pl.CostEstimate(flops=4 * 10**9, bytes_accessed=8 * 2**20, transcendentals=10**6),
        name="attend_inner",
    )(rows, counts, q, *(pltpu.with_memory_space_constraint(x, pltpu.HBM) for x in (g, own)))


def outer_kernel(unroll, sends_ref, rows_ref, counts_ref, q_ref, g_ref, own_ref, *refs):
    recv_refs, refs = refs[:LEVELS], refs[LEVELS + 3 :]
    att_ref, qg_ref, acc_ref = refs[:3]
    back_refs, refs = refs[3 : 3 + LEVELS], refs[3 + LEVELS :]
    far_ref, back_ref, staged, sems, back_sems = refs[0], refs[1], refs[2:4], refs[4], refs[5]
    outs = lambda i: row_copies(i, staged, (att_ref, qg_ref), sems)
    backs = [
        pltpu.make_async_copy(back_ref.at[b * PART : (b + 1) * PART, :], back_refs[b], back_sems.at[b])
        for b in range(LEVELS)
    ]
    for b in range(LEVELS):
        far_ref[b * PART : (b + 1) * PART, :] = recv_refs[b][...]

    def step(t, carry):
        blocks = []
        for u in range(unroll):
            e = t * unroll + u
            i = sends_ref[e // SEND, e % SEND]
            at = [rows_of(rows_ref[i, j]) if j != 1 else None for j in range(NNB)]
            far = (far_ref.at[rows_of(e), :], back_ref.at[rows_of(e), :])
            live = counts_ref[i] > NNB - 1
            blocks.append(staged_block(i, live, at, far, q_ref, g_ref, own_ref, acc_ref, staged, outs))
        run_staged(blocks)
        for b in range(LEVELS):
            pl.when(t == ((b + 1) * SEND - 1) // unroll)(backs[b].start)
        return carry

    lax.fori_loop(0, LEVELS * SEND // unroll, step, 0)

    def settle(e, carry):
        for copy in outs(sends_ref[e // SEND, e % SEND]):
            copy.wait()
        return carry

    lax.fori_loop(0, LEVELS * SEND, settle, 0)
    for copy in backs:
        copy.wait()


def outer(sends, rows, counts, q, g, own, recv, done):
    far = (LEVELS * PART, 2 * WIDE)
    return pl.pallas_call(
        functools.partial(outer_kernel, 10),
        out_shape=[
            pltpu.HBM((OWN, WIDE), BF16),
            pltpu.HBM((OWN, WIDE), BF16),
            pltpu.VMEM((OWN, 2 * WIDE), F32),
        ]
        + [pltpu.HBM((PART, 2 * WIDE), BF16)] * LEVELS,
        in_specs=[SM] * 3 + [VM] * (3 + LEVELS) + [HB, HB, VM],
        out_specs=[HB, HB, VM] + [HB] * LEVELS,
        scratch_shapes=[pltpu.VMEM(far, BF16), pltpu.VMEM(far, BF16)]
        + [pltpu.VMEM((OWN, WIDE), BF16)] * 2
        + [pltpu.SemaphoreType.DMA((2, NBLK)), pltpu.SemaphoreType.DMA((LEVELS,))],
        input_output_aliases={6 + LEVELS + n: n for n in range(3)},
        compiler_params=limits(16),
        cost_estimate=pl.CostEstimate(flops=8 * 10**9, bytes_accessed=8 * 2**20, transcendentals=2 * 10**6),
        name="attend_outer",
    )(sends, rows, counts, q, g, own, *recv, *done)


def join_kernel(sends_ref, acc_ref, *refs):
    arrived_refs = refs[:LEVELS]
    key_ref, value_ref = refs[LEVELS : LEVELS + 2]
    key_ref[...] = acc_ref[:, :WIDE].astype(BF16)
    value_ref[...] = acc_ref[:, WIDE:].astype(BF16)
    for b in range(LEVELS):
        for s in range(SEND):
            at = rows_of(sends_ref[b, s])
            both = acc_ref[at, :] + arrived_refs[b][s * BLK : (s + 1) * BLK, :].astype(F32)
            key_ref[at, :] = both[:, :WIDE].astype(BF16)
            value_ref[at, :] = both[:, WIDE:].astype(BF16)


def join(sends, acc, arrived):
    return pl.pallas_call(
        join_kernel,
        out_shape=[jax.ShapeDtypeStruct((OWN, WIDE), BF16)] * 2,
        in_specs=[SM] + [VM] * (1 + LEVELS),
        out_specs=[VM] * 2,
        compiler_params=limits(10),
        cost_estimate=pl.CostEstimate(flops=10**6, bytes_accessed=4 * 2**20, transcendentals=0),
        name="join_gradients",
    )(sends, acc, *arrived)


def body(query_rows, key_rows, value_rows, out_grad, boundary_send_blocks, neighbours, live_count):
    heads = lax.axis_size("head")
    mine = query_rows.shape[0]
    my_range = lax.axis_index("pix")
    sends = lax.dynamic_index_in_dim(boundary_send_blocks, my_range, 0, keepdims=False)
    rows = lax.dynamic_slice_in_dim(neighbours, my_range * NBLK, NBLK, 0)
    counts = lax.dynamic_slice_in_dim(live_count, my_range * NBLK, NBLK, 0)

    parts = split(key_rows, value_rows)
    parts = [shifted(x, *o) if o != (0, 0) else x for x, o in zip(parts, OFFSETS)]
    q = query_rows.reshape(mine, heads, WIDE).transpose(1, 0, 2)
    parts[0], rows, counts = lax.optimization_barrier((parts[0], rows, counts))
    own, *outgoing = pick(sends, parts)
    q, own = lax.optimization_barrier((q, own))
    q = lax.all_to_all(q, "head", 0, 0, tiled=True).reshape(OWN, WIDE)
    recv = [swapped(outgoing[b], b) for b in range(LEVELS)]
    *done, own, grad = inner(rows, counts, q, out_grad, own)
    attended, query_grad, acc, *back = outer(sends, rows, counts, q, grad, own, recv, done)
    arrived = [swapped(back[b], b) for b in range(LEVELS)]
    attended = lax.all_to_all(attended.reshape(heads, mine, WIDE), "head", 0, 0, tiled=True)
    attended = attended.transpose(1, 0, 2).reshape(mine, heads * WIDE)
    attended, arrived[0] = lax.optimization_barrier((attended, arrived[0]))
    key_grad, value_grad = join(sends, acc, arrived)
    return attended, query_grad, key_grad, value_grad


def solution(mesh):
    rows = P(("pix", "head"), None)
    split = P("pix", "head")
    return jax.shard_map(
        body,
        mesh=mesh,
        in_specs=(rows, rows, rows, split, P(), P(), P()),
        out_specs=(rows, split, split, split),
        check_vma=False,
    )
```

```python
import functools
import jax
import jax.numpy as jnp
from jax import lax
from jax.experimental import pallas as pl
from jax.experimental.pallas import tpu as pltpu
from jax.sharding import PartitionSpec as P

HD = 64
BLK = 64
NNB = 9
NBLK = 32
LEVELS = 5
SEND = 4
WIDE = 2 * HD
OWN = NBLK * BLK
PART = SEND * BLK
FILL = -1e30
CHUNKS = 8
LEVEL_GROUPS = ((0, 1, 2, 3, 4),)
HEAD_DEVICES = 8
OFFSETS = ((1, 0), (3, 0), (1, 1), (3, 1), (2, 0), (2, 1), (0, 1), (0, 0))
F32 = jnp.float32
BF16 = jnp.bfloat16

VM = pl.BlockSpec(memory_space=pltpu.VMEM)
SM = pl.BlockSpec(memory_space=pltpu.SMEM)
HB = pl.BlockSpec(memory_space=pltpu.HBM)


def swapped(block, bit):
    count = lax.axis_size("pix")
    route = [(low, low ^ (1 << bit)) for low in range(count)]
    return lax.ppermute(block, "pix", route)


def rows_of(start):
    return pl.ds(pl.multiple_of(start * BLK, BLK), BLK)


def offset_index(index, steps, core):
    chips = HEAD_DEVICES // 2
    return (index // 2 + steps) % chips * 2 + (index % 2 + core) % 2


def shifted(block, steps, core):
    route = [(i, offset_index(i, steps, core)) for i in range(HEAD_DEVICES)]
    return lax.ppermute(block, "head", route)


def limits(megabytes):
    return pltpu.CompilerParams(vmem_limit_bytes=megabytes * 2**20)


def split_kernel(key_ref, value_ref, *refs):
    parts, sems = refs[:-1], refs[-1]
    me = lax.axis_index("head")
    copies = []
    for t, (steps, core) in enumerate(OFFSETS):
        column = pl.ds(pl.multiple_of(offset_index(me, steps, core) * WIDE, WIDE), WIDE)
        for n, ref in enumerate((key_ref, value_ref)):
            copies.append(
                pltpu.make_async_copy(
                    ref.at[:, column], parts[t].at[:, n * WIDE : (n + 1) * WIDE], sems.at[2 * t + n]
                )
            )
    for copy in copies:
        copy.start()
    for copy in copies:
        copy.wait()


def split(keys, values):
    mine = keys.shape[0]
    return pl.pallas_call(
        split_kernel,
        out_shape=[pltpu.VMEM((mine, 2 * WIDE), BF16)] * HEAD_DEVICES,
        in_specs=[HB] * 2,
        out_specs=[VM] * HEAD_DEVICES,
        scratch_shapes=[pltpu.SemaphoreType.DMA((2 * HEAD_DEVICES,))],
        compiler_params=limits(4),
        cost_estimate=pl.CostEstimate(flops=0, bytes_accessed=2 * 2**20, transcendentals=0),
        name="split_keys_values",
    )(pltpu.with_memory_space_constraint(keys, pltpu.HBM), pltpu.with_memory_space_constraint(values, pltpu.HBM))


def gather_parts(parts, held_ref):
    me = lax.axis_index("head")
    mine = OWN // HEAD_DEVICES
    for part, (steps, core) in zip(parts, OFFSETS):
        source = offset_index(me, HEAD_DEVICES // 2 - steps, core)
        held_ref[pl.ds(pl.multiple_of(source * mine, mine), mine), :] = part[...]


def pick_kernel(sends_ref, *refs):
    parts, out_refs, held_ref = refs[:HEAD_DEVICES], refs[HEAD_DEVICES:-1], refs[-1]
    gather_parts(parts, held_ref)
    for b in range(LEVELS):
        for s in range(SEND):
            out_refs[b][s * BLK : (s + 1) * BLK, :] = held_ref[rows_of(sends_ref[b, s]), :]


def pick(sends, parts):
    return pl.pallas_call(
        pick_kernel,
        out_shape=[pltpu.VMEM((PART, 2 * WIDE), BF16)] * LEVELS,
        in_specs=[SM] + [VM] * HEAD_DEVICES,
        out_specs=[VM] * LEVELS,
        scratch_shapes=[pltpu.VMEM((OWN, 2 * WIDE), BF16)],
        compiler_params=limits(8),
        cost_estimate=pl.CostEstimate(flops=0, bytes_accessed=4 * 2**20, transcendentals=0),
        name="pick_boundary",
    )(sends, *parts)


def staged_block(i, live, at, far, q_ref, g_ref, own_ref, acc_ref, staged, outs):
    rows = rows_of(i)
    q = q_ref[rows, :] * jnp.array(HD**-0.5, BF16)
    g = g_ref[rows, :]
    low = lax.broadcasted_iota(jnp.int32, (BLK, WIDE), 1) < HD
    z = jnp.zeros((BLK, WIDE), BF16)
    q = jnp.concatenate([jnp.where(low, q, z), jnp.where(low, z, q)], 0)
    g = jnp.concatenate([jnp.where(low, g, z), jnp.where(low, z, g)], 0)
    blocks = [own_ref[a, :] if a is not None else far[0][...] for a in at]
    kv = jnp.concatenate(blocks, 0)
    product = functools.partial(lax.dot_general, preferred_element_type=F32)
    across, plain, down = (((1,), (1,)), ((), ())), (((1,), (0,)), ((), ())), (((0,), (0,)), ((), ()))
    s = product(kv[:, :WIDE], q, across)
    d = product(kv[:, WIDE:], g, across)
    yield
    s = [s[j * BLK : (j + 1) * BLK] for j in range(NNB)]
    d = [d[j * BLK : (j + 1) * BLK] for j in range(NNB)]
    s[-1] = jnp.where(live, s[-1], FILL)
    peak = jnp.max(functools.reduce(jnp.maximum, s), 0, keepdims=True)
    p = [jnp.exp(x - peak) for x in s]
    total = jnp.sum(sum(p[1:], p[0]), 0, keepdims=True)
    dot = [x * y for x, y in zip(p, d)]
    inv = 1.0 / total
    dot = jnp.sum(sum(dot[1:], dot[0]), 0, keepdims=True) * inv
    weights = [x * inv for x in p]
    rounded = jnp.concatenate([x.astype(BF16) for x in weights], 0)
    grads = jnp.concatenate([(x * (y - dot)).astype(BF16) for x, y in zip(weights, d)], 0)
    yield
    terms = jnp.concatenate([product(grads, q, plain), product(rounded, g, plain)], 1)
    for j in range(NNB):
        term = terms[j * BLK : (j + 1) * BLK]
        if at[j] is None:
            far[1][...] = term.astype(BF16)
        else:
            acc_ref[at[j], :] += term
    yield
    results = product(jnp.concatenate([grads, rounded], 1), kv, down)
    qg, att = results[:WIDE, :WIDE], results[WIDE:, WIDE:]
    staged[0][rows, :] = jnp.where(low, att[:BLK], att[BLK:]).astype(BF16)
    staged[1][rows, :] = (jnp.where(low, qg[:BLK], qg[BLK:]) * HD**-0.5).astype(BF16)
    for copy in outs(i):
        copy.start()
    yield


def run_staged(blocks, ready=None):
    stages = 4
    for t in range(len(blocks) + stages - 1):
        for k in reversed(range(stages)):
            if 0 <= t - k < len(blocks):
                next(blocks[t - k])
                if ready and k == 2 and t - k in ready:
                    ready[t - k].start()


def row_copies(at, staged, outs, sems):
    return [
        pltpu.make_async_copy(x.at[rows_of(at), :], y.at[rows_of(at), :], sems.at[n, at])
        for n, (x, y) in enumerate(zip(staged, outs))
    ]


def inner_kernel(unroll, rows_ref, counts_ref, q_ref, far_g_ref, *refs):
    parts, refs = refs[:HEAD_DEVICES], refs[HEAD_DEVICES:]
    att_ref, qg_ref, acc_ref, own_ref, g_ref, list_ref = refs[:6]
    staged, sems, in_sems = refs[6:8], refs[8], refs[9]
    loads = []
    for c in range(CHUNKS):
        part = pl.ds(c * (OWN // CHUNKS), OWN // CHUNKS)
        loads.append(pltpu.make_async_copy(far_g_ref.at[part, :], g_ref.at[part, :], in_sems.at[c]))
        loads[-1].start()
    gather_parts(parts, own_ref)
    outs = lambda i: row_copies(i, staged, (att_ref, qg_ref), sems)
    steps = NBLK - LEVELS * SEND
    acc_ref[...] = jnp.zeros_like(acc_ref)

    def note(i, count):
        list_ref[count] = i
        return count + (rows_ref[i, 1] < NBLK).astype(jnp.int32)

    lax.fori_loop(0, NBLK, note, jnp.int32(0))
    for load in loads:
        load.wait()

    def step(t, carry):
        blocks = []
        for u in range(unroll):
            i = list_ref[t * unroll + u]
            at = [rows_of(rows_ref[i, j]) for j in range(NNB)]
            live = counts_ref[i] > NNB - 1
            blocks.append(staged_block(i, live, at, None, q_ref, g_ref, own_ref, acc_ref, staged, outs))
        run_staged(blocks)
        return carry

    lax.fori_loop(0, steps // unroll, step, 0)

    def settle(t, carry):
        for copy in outs(list_ref[t]):
            copy.wait()
        return carry

    lax.fori_loop(0, steps, settle, 0)


def inner(rows, counts, q, g, parts):
    return pl.pallas_call(
        functools.partial(inner_kernel, 12),
        out_shape=[
            pltpu.HBM((OWN, WIDE), BF16),
            pltpu.HBM((OWN, WIDE), BF16),
            pltpu.VMEM((OWN, 2 * WIDE), F32),
            pltpu.VMEM((OWN, 2 * WIDE), BF16),
            pltpu.VMEM((OWN, WIDE), BF16),
        ],
        in_specs=[SM, SM, VM, HB] + [VM] * HEAD_DEVICES,
        out_specs=[HB, HB, VM, VM, VM],
        scratch_shapes=[pltpu.SMEM((NBLK + 1,), jnp.int32)]
        + [pltpu.VMEM((OWN, WIDE), BF16)] * 2
        + [pltpu.SemaphoreType.DMA((2, NBLK)), pltpu.SemaphoreType.DMA((CHUNKS,))],
        compiler_params=limits(16),
        cost_estimate=pl.CostEstimate(flops=4 * 10**9, bytes_accessed=8 * 2**20, transcendentals=10**6),
        name="attend_inner",
    )(rows, counts, q, pltpu.with_memory_space_constraint(g, pltpu.HBM), *parts)


def outer_kernel(levels, sends_ref, rows_ref, counts_ref, q_ref, g_ref, own_ref, *refs):
    recv_refs, refs = refs[: len(levels)], refs[len(levels) + 3 :]
    att_ref, qg_ref, acc_ref = refs[:3]
    back_refs, refs = refs[3 : 3 + len(levels)], refs[3 + len(levels) :]
    held, staged, sems, back_sems = refs[: len(levels)], refs[-4:-2], refs[-2], refs[-1]
    outs = lambda i: row_copies(i, staged, (att_ref, qg_ref), sems)
    backs = [pltpu.make_async_copy(x, y, back_sems.at[n]) for n, (x, y) in enumerate(zip(held, back_refs))]
    blocks, ready = [], {}
    for n, b in enumerate(levels):
        for s in range(SEND):
            i = sends_ref[b, s]
            at = [rows_of(rows_ref[i, j]) if j != 1 else None for j in range(NNB)]
            place = slice(s * BLK, (s + 1) * BLK)
            far = (recv_refs[n].at[place, :], held[n].at[place, :])
            live = counts_ref[i] > NNB - 1
            blocks.append(staged_block(i, live, at, far, q_ref, g_ref, own_ref, acc_ref, staged, outs))
        ready[len(blocks) - 1] = backs[n]
    run_staged(blocks, ready)
    for b in levels:
        for s in range(SEND):
            for copy in outs(sends_ref[b, s]):
                copy.wait()
    for copy in backs:
        copy.wait()


def outer(levels, sends, rows, counts, q, g, own, recv, done):
    recv = [recv[b] for b in levels]
    return pl.pallas_call(
        functools.partial(outer_kernel, levels),
        out_shape=[
            pltpu.HBM((OWN, WIDE), BF16),
            pltpu.HBM((OWN, WIDE), BF16),
            pltpu.VMEM((OWN, 2 * WIDE), F32),
        ]
        + [pltpu.HBM((PART, 2 * WIDE), BF16)] * len(levels),
        in_specs=[SM] * 3 + [VM] * (3 + len(levels)) + [HB, HB, VM],
        out_specs=[HB, HB, VM] + [HB] * len(levels),
        scratch_shapes=[pltpu.VMEM((PART, 2 * WIDE), BF16)] * len(levels)
        + [pltpu.VMEM((OWN, WIDE), BF16)] * 2
        + [pltpu.SemaphoreType.DMA((2, NBLK)), pltpu.SemaphoreType.DMA((len(levels),))],
        input_output_aliases={6 + len(levels) + n: n for n in range(3)},
        compiler_params=limits(16),
        cost_estimate=pl.CostEstimate(flops=4 * 10**9, bytes_accessed=4 * 2**20, transcendentals=10**6),
        name="attend_outer",
    )(sends, rows, counts, q, g, own, *recv, *done)


def join_kernel(sends_ref, acc_ref, *refs):
    arrived_refs, refs = refs[:LEVELS], refs[LEVELS:]
    outs, sum_ref, staged, sems = refs[:2], refs[2], refs[3:5], refs[5]
    sum_ref[...] = acc_ref[...]
    for b in range(LEVELS):
        for s in range(SEND):
            sum_ref[rows_of(sends_ref[b, s]), :] += arrived_refs[b][s * BLK : (s + 1) * BLK, :].astype(F32)
    copies = []
    for c in range(CHUNKS):
        part = pl.ds(c * (OWN // CHUNKS), OWN // CHUNKS)
        for n in range(2):
            staged[n][part, :] = sum_ref[part, n * WIDE : (n + 1) * WIDE].astype(BF16)
            copies.append(pltpu.make_async_copy(staged[n].at[part, :], outs[n].at[part, :], sems.at[n, c]))
            copies[-1].start()
    for copy in copies:
        copy.wait()


def join(sends, acc, arrived):
    return pl.pallas_call(
        join_kernel,
        out_shape=[pltpu.HBM((OWN, WIDE), BF16)] * 2,
        in_specs=[SM] + [VM] * (1 + LEVELS),
        out_specs=[HB] * 2,
        scratch_shapes=[pltpu.VMEM((OWN, 2 * WIDE), F32)]
        + [pltpu.VMEM((OWN, WIDE), BF16)] * 2
        + [pltpu.SemaphoreType.DMA((2, CHUNKS))],
        compiler_params=limits(10),
        cost_estimate=pl.CostEstimate(flops=10**6, bytes_accessed=4 * 2**20, transcendentals=0),
        name="join_gradients",
    )(sends, acc, *arrived)


def body(query_rows, key_rows, value_rows, out_grad, boundary_send_blocks, neighbours, live_count):
    heads = lax.axis_size("head")
    mine = query_rows.shape[0]
    my_range = lax.axis_index("pix")
    sends = lax.dynamic_index_in_dim(boundary_send_blocks, my_range, 0, keepdims=False)
    rows = lax.dynamic_slice_in_dim(neighbours, my_range * NBLK, NBLK, 0)
    counts = lax.dynamic_slice_in_dim(live_count, my_range * NBLK, NBLK, 0)

    parts = split(key_rows, value_rows)
    parts = [shifted(x, *o) if o != (0, 0) else x for x, o in zip(parts, OFFSETS)]
    q = query_rows.reshape(mine, heads, WIDE).transpose(1, 0, 2)
    parts[0], rows, counts = lax.optimization_barrier((parts[0], rows, counts))
    outgoing = pick(sends, parts)
    q, outgoing = lax.optimization_barrier((q, outgoing))
    q = lax.all_to_all(q, "head", 0, 0, tiled=True).reshape(OWN, WIDE)
    recv = [swapped(outgoing[b], b) for b in range(LEVELS)]
    *done, own, grad = inner(rows, counts, q, out_grad, parts)
    arrived = []
    for levels in LEVEL_GROUPS:
        done = outer(levels, sends, rows, counts, q, grad, own, recv, done)
        arrived += [swapped(x, b) for x, b in zip(done[3:], levels)]
        done = done[:3]
    attended, query_grad, acc = done
    attended = lax.all_to_all(attended.reshape(heads, mine, WIDE), "head", 0, 0, tiled=True)
    attended = attended.transpose(1, 0, 2).reshape(mine, heads * WIDE)
    attended, arrived[0] = lax.optimization_barrier((attended, arrived[0]))
    key_grad, value_grad = join(sends, acc, arrived)
    return attended, query_grad, key_grad, value_grad


def solution(mesh):
    rows = P(("pix", "head"), None)
    split = P("pix", "head")
    return jax.shard_map(
        body,
        mesh=mesh,
        in_specs=(rows, rows, rows, split, P(), P(), P()),
        out_specs=(rows, split, split, split),
        check_vma=False,
    )
```

```python
import functools
import jax
import jax.numpy as jnp
from jax import lax
from jax.experimental import pallas as pl
from jax.experimental.pallas import tpu as pltpu
from jax.sharding import PartitionSpec as P

HD = 64
BLK = 64
NNB = 9
NBLK = 32
LEVELS = 5
SEND = 4
WIDE = 2 * HD
OWN = NBLK * BLK
PART = SEND * BLK
FILL = -1e30
CHUNKS = 8
HEAD_DEVICES = 8
OFFSETS = ((1, 0), (3, 0), (1, 1), (3, 1), (2, 0), (2, 1), (0, 1), (0, 0))
F32 = jnp.float32
BF16 = jnp.bfloat16

VM = pl.BlockSpec(memory_space=pltpu.VMEM)
HB = pl.BlockSpec(memory_space=pltpu.HBM)


def swapped(block, bit):
    count = lax.axis_size("pix")
    route = [(low, low ^ (1 << bit)) for low in range(count)]
    return lax.ppermute(block, "pix", route)


def rows_of(start):
    return pl.ds(pl.multiple_of(start * BLK, BLK), BLK)


def offset_index(index, steps, core):
    chips = HEAD_DEVICES // 2
    return (index // 2 + steps) % chips * 2 + (index % 2 + core) % 2


def shifted(block, steps, core):
    route = [(i, offset_index(i, steps, core)) for i in range(HEAD_DEVICES)]
    return lax.ppermute(block, "head", route)


def limits(megabytes):
    return pltpu.CompilerParams(vmem_limit_bytes=megabytes * 2**20)


def split_kernel(key_ref, value_ref, *refs):
    parts, sems = refs[:-1], refs[-1]
    me = lax.axis_index("head")
    copies = []
    for t, (steps, core) in enumerate(OFFSETS):
        column = pl.ds(pl.multiple_of(offset_index(me, steps, core) * WIDE, WIDE), WIDE)
        for n, ref in enumerate((key_ref, value_ref)):
            copies.append(
                pltpu.make_async_copy(
                    ref.at[:, column], parts[t].at[:, n * WIDE : (n + 1) * WIDE], sems.at[2 * t + n]
                )
            )
    for copy in copies:
        copy.start()
    for copy in copies:
        copy.wait()


def split(keys, values):
    mine = keys.shape[0]
    return pl.pallas_call(
        split_kernel,
        out_shape=[pltpu.VMEM((mine, 2 * WIDE), BF16)] * HEAD_DEVICES,
        in_specs=[HB] * 2,
        out_specs=[VM] * HEAD_DEVICES,
        scratch_shapes=[pltpu.SemaphoreType.DMA((2 * HEAD_DEVICES,))],
        compiler_params=limits(4),
        cost_estimate=pl.CostEstimate(flops=0, bytes_accessed=2 * 2**20, transcendentals=0),
        name="split_keys_values",
    )(pltpu.with_memory_space_constraint(keys, pltpu.HBM), pltpu.with_memory_space_constraint(values, pltpu.HBM))


def index_loads(sources, targets, sems):
    loads = [pltpu.make_async_copy(x, y, sems.at[n]) for n, (x, y) in enumerate(zip(sources, targets))]
    for load in loads:
        load.start()
    return loads


def in_hbm(*arrays):
    return [pltpu.with_memory_space_constraint(x, pltpu.HBM) for x in arrays]


def index_scratch(*arrays):
    return [pltpu.SMEM(x.shape, x.dtype) for x in arrays] + [pltpu.SemaphoreType.DMA((len(arrays),))]


def pick_kernel(far_sends_ref, *refs):
    parts, refs = refs[:HEAD_DEVICES], refs[HEAD_DEVICES:]
    own_ref, out_refs, held_ref, sems = refs[0], refs[1 : 1 + LEVELS], refs[-4], refs[-3]
    sends_ref, index_sems = refs[-2:]
    (index,) = index_loads((far_sends_ref,), (sends_ref,), index_sems)
    me = lax.axis_index("head")
    mine = OWN // HEAD_DEVICES
    copies = []
    for t, (steps, core) in enumerate(OFFSETS):
        source = offset_index(me, HEAD_DEVICES // 2 - steps, core)
        at = pl.ds(pl.multiple_of(source * mine, mine), mine)
        copies.append(pltpu.make_async_copy(parts[t], own_ref.at[at, :], sems.at[t]))
        copies[-1].start()
        held_ref[at, :] = parts[t][...]
    index.wait()
    for b in range(LEVELS):
        for s in range(SEND):
            out_refs[b][s * BLK : (s + 1) * BLK, :] = held_ref[rows_of(sends_ref[b, s]), :]
    for copy in copies:
        copy.wait()


def pick(sends, parts):
    return pl.pallas_call(
        pick_kernel,
        out_shape=[pltpu.HBM((OWN, 2 * WIDE), BF16)] + [pltpu.VMEM((PART, 2 * WIDE), BF16)] * LEVELS,
        in_specs=[HB] + [VM] * HEAD_DEVICES,
        out_specs=[HB] + [VM] * LEVELS,
        scratch_shapes=[pltpu.VMEM((OWN, 2 * WIDE), BF16), pltpu.SemaphoreType.DMA((HEAD_DEVICES,))]
        + index_scratch(sends),
        compiler_params=limits(8),
        cost_estimate=pl.CostEstimate(flops=0, bytes_accessed=4 * 2**20, transcendentals=0),
        name="pick_boundary",
    )(*in_hbm(sends), *parts)


def staged_block(i, live, at, far, q_ref, g_ref, own_ref, acc_ref, staged, outs):
    rows = rows_of(i)
    q = q_ref[rows, :] * jnp.array(HD**-0.5, BF16)
    g = g_ref[rows, :]
    low = lax.broadcasted_iota(jnp.int32, (BLK, WIDE), 1) < HD
    z = jnp.zeros((BLK, WIDE), BF16)
    q = jnp.concatenate([jnp.where(low, q, z), jnp.where(low, z, q)], 0)
    g = jnp.concatenate([jnp.where(low, g, z), jnp.where(low, z, g)], 0)
    blocks = [own_ref[a, :] if a is not None else far[0][...] for a in at]
    kv = jnp.concatenate(blocks, 0)
    product = functools.partial(lax.dot_general, preferred_element_type=F32)
    across, plain, down = (((1,), (1,)), ((), ())), (((1,), (0,)), ((), ())), (((0,), (0,)), ((), ()))
    s = product(kv[:, :WIDE], q, across)
    d = product(kv[:, WIDE:], g, across)
    yield
    s = [s[j * BLK : (j + 1) * BLK] for j in range(NNB)]
    d = [d[j * BLK : (j + 1) * BLK] for j in range(NNB)]
    s[-1] = jnp.where(live, s[-1], FILL)
    peak = jnp.max(functools.reduce(jnp.maximum, s), 0, keepdims=True)
    p = [jnp.exp(x - peak) for x in s]
    total = jnp.sum(sum(p[1:], p[0]), 0, keepdims=True)
    dot = [x * y for x, y in zip(p, d)]
    inv = 1.0 / total
    dot = jnp.sum(sum(dot[1:], dot[0]), 0, keepdims=True) * inv
    weights = [x * inv for x in p]
    rounded = jnp.concatenate([x.astype(BF16) for x in weights], 0)
    grads = jnp.concatenate([(x * (y - dot)).astype(BF16) for x, y in zip(weights, d)], 0)
    yield
    terms = jnp.concatenate([product(grads, q, plain), product(rounded, g, plain)], 1)
    for j in range(NNB):
        term = terms[j * BLK : (j + 1) * BLK]
        if at[j] is None:
            far[1][...] = term.astype(BF16)
        else:
            acc_ref[at[j], :] += term
    yield
    results = product(jnp.concatenate([grads, rounded], 1), kv, down)
    qg, att = results[:WIDE, :WIDE], results[WIDE:, WIDE:]
    staged[0][rows, :] = jnp.where(low, att[:BLK], att[BLK:]).astype(BF16)
    staged[1][rows, :] = (jnp.where(low, qg[:BLK], qg[BLK:]) * HD**-0.5).astype(BF16)
    for copy in outs(i):
        copy.start()
    yield


def run_staged(blocks, ready=None):
    stages = 4
    for t in range(len(blocks) + stages - 1):
        for k in reversed(range(stages)):
            if 0 <= t - k < len(blocks):
                next(blocks[t - k])
                if ready and k == 2 and t - k in ready:
                    ready[t - k].start()


def row_copies(at, staged, outs, sems):
    return [
        pltpu.make_async_copy(x.at[rows_of(at), :], y.at[rows_of(at), :], sems.at[n, at])
        for n, (x, y) in enumerate(zip(staged, outs))
    ]


def inner_kernel(unroll, far_rows_ref, far_counts_ref, q_ref, far_g_ref, far_own_ref, *refs):
    att_ref, qg_ref, acc_ref, own_ref, g_ref, list_ref = refs[:6]
    staged, sems, in_sems = refs[6:8], refs[8], refs[9]
    rows_ref, counts_ref, index_sems = refs[10:]
    indices = index_loads((far_rows_ref, far_counts_ref), (rows_ref, counts_ref), index_sems)
    loads = []
    for n, (x, y) in enumerate(((far_own_ref, own_ref), (far_g_ref, g_ref))):
        for c in range(CHUNKS):
            part = pl.ds(c * (OWN // CHUNKS), OWN // CHUNKS)
            loads.append(pltpu.make_async_copy(x.at[part, :], y.at[part, :], in_sems.at[n, c]))
            loads[-1].start()
    outs = lambda i: row_copies(i, staged, (att_ref, qg_ref), sems)
    steps = NBLK - LEVELS * SEND
    acc_ref[...] = jnp.zeros_like(acc_ref)

    for load in indices:
        load.wait()

    def note(i, count):
        list_ref[count] = i
        return count + (rows_ref[i, 1] < NBLK).astype(jnp.int32)

    lax.fori_loop(0, NBLK, note, jnp.int32(0))
    for load in loads:
        load.wait()

    def step(t, carry):
        blocks = []
        for u in range(unroll):
            i = list_ref[t * unroll + u]
            at = [rows_of(rows_ref[i, j]) for j in range(NNB)]
            live = counts_ref[i] > NNB - 1
            blocks.append(staged_block(i, live, at, None, q_ref, g_ref, own_ref, acc_ref, staged, outs))
        run_staged(blocks)
        return carry

    lax.fori_loop(0, steps // unroll, step, 0)

    def settle(t, carry):
        for copy in outs(list_ref[t]):
            copy.wait()
        return carry

    lax.fori_loop(0, steps, settle, 0)


def inner(rows, counts, q, g, own):
    return pl.pallas_call(
        functools.partial(inner_kernel, 12),
        out_shape=[
            pltpu.HBM((OWN, WIDE), BF16),
            pltpu.HBM((OWN, WIDE), BF16),
            pltpu.VMEM((OWN, 2 * WIDE), F32),
            pltpu.VMEM((OWN, 2 * WIDE), BF16),
            pltpu.VMEM((OWN, WIDE), BF16),
        ],
        in_specs=[HB, HB, VM, HB, HB],
        out_specs=[HB, HB, VM, VM, VM],
        scratch_shapes=[pltpu.SMEM((NBLK + 1,), jnp.int32)]
        + [pltpu.VMEM((OWN, WIDE), BF16)] * 2
        + [pltpu.SemaphoreType.DMA((2, NBLK)), pltpu.SemaphoreType.DMA((2, CHUNKS))]
        + index_scratch(rows, counts),
        compiler_params=limits(16),
        cost_estimate=pl.CostEstimate(flops=4 * 10**9, bytes_accessed=8 * 2**20, transcendentals=10**6),
        name="attend_inner",
    )(*in_hbm(rows, counts), q, *in_hbm(g, own))


def outer_kernel(levels, far_sends_ref, far_rows_ref, far_counts_ref, q_ref, g_ref, own_ref, *refs):
    recv_refs, refs = refs[: len(levels)], refs[len(levels) + 3 :]
    sends_ref, rows_ref, counts_ref, index_sems = refs[-4:]
    refs = refs[:-4]
    indices = index_loads(
        (far_sends_ref, far_rows_ref, far_counts_ref), (sends_ref, rows_ref, counts_ref), index_sems
    )
    for load in indices:
        load.wait()
    att_ref, qg_ref, acc_ref = refs[:3]
    back_refs, refs = refs[3 : 3 + len(levels)], refs[3 + len(levels) :]
    held, staged, sems, back_sems = refs[: len(levels)], refs[-4:-2], refs[-2], refs[-1]
    outs = lambda i: row_copies(i, staged, (att_ref, qg_ref), sems)
    backs = [pltpu.make_async_copy(x, y, back_sems.at[n]) for n, (x, y) in enumerate(zip(held, back_refs))]
    blocks, ready = [], {}
    for n, b in enumerate(levels):
        for s in range(SEND):
            i = sends_ref[b, s]
            at = [rows_of(rows_ref[i, j]) if j != 1 else None for j in range(NNB)]
            place = slice(s * BLK, (s + 1) * BLK)
            far = (recv_refs[n].at[place, :], held[n].at[place, :])
            live = counts_ref[i] > NNB - 1
            blocks.append(staged_block(i, live, at, far, q_ref, g_ref, own_ref, acc_ref, staged, outs))
        ready[len(blocks) - 1] = backs[n]
    run_staged(blocks, ready)
    for b in levels:
        for s in range(SEND):
            for copy in outs(sends_ref[b, s]):
                copy.wait()
    for copy in backs:
        copy.wait()


def outer(levels, sends, rows, counts, q, g, own, recv, done):
    recv = [recv[b] for b in levels]
    return pl.pallas_call(
        functools.partial(outer_kernel, levels),
        out_shape=[
            pltpu.HBM((OWN, WIDE), BF16),
            pltpu.HBM((OWN, WIDE), BF16),
            pltpu.VMEM((OWN, 2 * WIDE), F32),
        ]
        + [pltpu.HBM((PART, 2 * WIDE), BF16)] * len(levels),
        in_specs=[HB] * 3 + [VM] * (3 + len(levels)) + [HB, HB, VM],
        out_specs=[HB, HB, VM] + [HB] * len(levels),
        scratch_shapes=[pltpu.VMEM((PART, 2 * WIDE), BF16)] * len(levels)
        + [pltpu.VMEM((OWN, WIDE), BF16)] * 2
        + [pltpu.SemaphoreType.DMA((2, NBLK)), pltpu.SemaphoreType.DMA((len(levels),))]
        + index_scratch(sends, rows, counts),
        input_output_aliases={6 + len(levels) + n: n for n in range(3)},
        compiler_params=limits(16),
        cost_estimate=pl.CostEstimate(flops=4 * 10**9, bytes_accessed=4 * 2**20, transcendentals=10**6),
        name="attend_outer",
    )(*in_hbm(sends, rows, counts), q, g, own, *recv, *done)


def join_kernel(far_sends_ref, acc_ref, *refs):
    sends_ref, index_sems = refs[-2:]
    (index,) = index_loads((far_sends_ref,), (sends_ref,), index_sems)
    arrived_refs = refs[:LEVELS]
    key_ref, value_ref = refs[LEVELS : LEVELS + 2]
    key_ref[...] = acc_ref[:, :WIDE].astype(BF16)
    value_ref[...] = acc_ref[:, WIDE:].astype(BF16)
    index.wait()
    for b in range(LEVELS):
        for s in range(SEND):
            at = rows_of(sends_ref[b, s])
            both = acc_ref[at, :] + arrived_refs[b][s * BLK : (s + 1) * BLK, :].astype(F32)
            key_ref[at, :] = both[:, :WIDE].astype(BF16)
            value_ref[at, :] = both[:, WIDE:].astype(BF16)


def join(sends, acc, arrived):
    return pl.pallas_call(
        join_kernel,
        out_shape=[jax.ShapeDtypeStruct((OWN, WIDE), BF16)] * 2,
        in_specs=[HB] + [VM] * (1 + LEVELS),
        out_specs=[VM] * 2,
        scratch_shapes=index_scratch(sends),
        compiler_params=limits(10),
        cost_estimate=pl.CostEstimate(flops=10**6, bytes_accessed=4 * 2**20, transcendentals=0),
        name="join_gradients",
    )(*in_hbm(sends), acc, *arrived)


def body(query_rows, key_rows, value_rows, out_grad, boundary_send_blocks, neighbours, live_count):
    heads = lax.axis_size("head")
    mine = query_rows.shape[0]
    my_range = lax.axis_index("pix")
    sends = lax.dynamic_index_in_dim(boundary_send_blocks, my_range, 0, keepdims=False)
    rows = lax.dynamic_slice_in_dim(neighbours, my_range * NBLK, NBLK, 0)
    counts = lax.dynamic_slice_in_dim(live_count, my_range * NBLK, NBLK, 0)

    parts = split(key_rows, value_rows)
    parts = [shifted(x, *o) if o != (0, 0) else x for x, o in zip(parts, OFFSETS)]
    q = query_rows.reshape(mine, heads, WIDE).transpose(1, 0, 2)
    parts[0], rows, counts = lax.optimization_barrier((parts[0], rows, counts))
    own, *outgoing = pick(sends, parts)
    q, own = lax.optimization_barrier((q, own))
    q = lax.all_to_all(q, "head", 0, 0, tiled=True).reshape(OWN, WIDE)
    recv = [swapped(outgoing[b], b) for b in range(LEVELS)]
    *done, own, grad = inner(rows, counts, q, out_grad, own)
    levels = tuple(range(LEVELS))
    attended, query_grad, acc, *back = outer(levels, sends, rows, counts, q, grad, own, recv, done)
    arrived = [swapped(back[b], b) for b in range(LEVELS)]
    attended = lax.all_to_all(attended.reshape(heads, mine, WIDE), "head", 0, 0, tiled=True)
    attended = attended.transpose(1, 0, 2).reshape(mine, heads * WIDE)
    attended, arrived[0] = lax.optimization_barrier((attended, arrived[0]))
    key_grad, value_grad = join(sends, acc, arrived)
    return attended, query_grad, key_grad, value_grad


def solution(mesh):
    rows = P(("pix", "head"), None)
    split = P("pix", "head")
    return jax.shard_map(
        body,
        mesh=mesh,
        in_specs=(rows, rows, rows, split, P(), P(), P()),
        out_specs=(rows, split, split, split),
        check_vma=False,
    )
```

```python
import functools
import jax
import jax.numpy as jnp
from jax import lax
from jax.experimental import pallas as pl
from jax.experimental.pallas import tpu as pltpu
from jax.sharding import PartitionSpec as P

HD = 64
BLK = 64
NNB = 9
NBLK = 32
LEVELS = 5
SEND = 4
WIDE = 2 * HD
OWN = NBLK * BLK
PART = SEND * BLK
FILL = -1e30
CHUNKS = 8
LANES = 128
HEAD_DEVICES = 8
OFFSETS = ((1, 0), (3, 0), (1, 1), (3, 1), (2, 0), (2, 1), (0, 1), (0, 0))
F32 = jnp.float32
BF16 = jnp.bfloat16

VM = pl.BlockSpec(memory_space=pltpu.VMEM)
HB = pl.BlockSpec(memory_space=pltpu.HBM)


def swapped(block, bit):
    count = lax.axis_size("pix")
    route = [(low, low ^ (1 << bit)) for low in range(count)]
    return lax.ppermute(block, "pix", route)


def rows_of(start):
    return pl.ds(pl.multiple_of(start * BLK, BLK), BLK)


def offset_index(index, steps, core):
    chips = HEAD_DEVICES // 2
    return (index // 2 + steps) % chips * 2 + (index % 2 + core) % 2


def shifted(block, steps, core):
    route = [(i, offset_index(i, steps, core)) for i in range(HEAD_DEVICES)]
    return lax.ppermute(block, "head", route)


def limits(megabytes):
    return pltpu.CompilerParams(vmem_limit_bytes=megabytes * 2**20)


def split_kernel(key_ref, value_ref, *refs):
    parts, sems = refs[:-1], refs[-1]
    me = lax.axis_index("head")
    copies = []
    for t, (steps, core) in enumerate(OFFSETS):
        column = pl.ds(pl.multiple_of(offset_index(me, steps, core) * WIDE, WIDE), WIDE)
        for n, ref in enumerate((key_ref, value_ref)):
            copies.append(
                pltpu.make_async_copy(
                    ref.at[:, column], parts[t].at[:, n * WIDE : (n + 1) * WIDE], sems.at[2 * t + n]
                )
            )
    for copy in copies:
        copy.start()
    for copy in copies:
        copy.wait()


def split(keys, values):
    mine = keys.shape[0]
    return pl.pallas_call(
        split_kernel,
        out_shape=[pltpu.VMEM((mine, 2 * WIDE), BF16)] * HEAD_DEVICES,
        in_specs=[HB] * 2,
        out_specs=[VM] * HEAD_DEVICES,
        scratch_shapes=[pltpu.SemaphoreType.DMA((2 * HEAD_DEVICES,))],
        compiler_params=limits(4),
        cost_estimate=pl.CostEstimate(flops=0, bytes_accessed=2 * 2**20, transcendentals=0),
        name="split_keys_values",
    )(pltpu.with_memory_space_constraint(keys, pltpu.HBM), pltpu.with_memory_space_constraint(values, pltpu.HBM))


class Table:
    def __init__(self, ref, place):
        self.ref, self.place = ref, place

    def __getitem__(self, index):
        return self.ref[self.place(*index) if isinstance(index, tuple) else self.place(index)]


def sends_load(whole_ref, held_ref, sem):
    load = pltpu.make_async_copy(whole_ref, held_ref, sem)
    load.start()
    mine = lax.axis_index("pix")
    return load, Table(held_ref, lambda b, s: (b, s, mine))


def rows_load(whole_ref, held_ref, sem):
    mine = lax.axis_index("pix")
    per = LANES // NBLK
    columns = pl.ds(pl.multiple_of(mine // per * LANES, LANES), LANES)
    load = pltpu.make_async_copy(whole_ref.at[:, columns], held_ref, sem)
    load.start()
    return load, Table(held_ref, lambda i, j: (j, mine % per * NBLK + i))


def counts_load(whole_ref, held_ref, sem):
    load = pltpu.make_async_copy(whole_ref, held_ref, sem)
    load.start()
    mine = lax.axis_index("pix")
    return load, Table(held_ref, lambda i: mine * NBLK + i)


def sends_scratch(sends):
    return [pltpu.SMEM(sends.shape, jnp.int32), pltpu.SemaphoreType.DMA]


def block_scratch(counts):
    return [
        pltpu.SMEM((NNB, LANES), jnp.int32),
        pltpu.SMEM(counts.shape, jnp.int32),
        pltpu.SemaphoreType.DMA((2,)),
    ]


def in_hbm(*arrays):
    return [pltpu.with_memory_space_constraint(x, pltpu.HBM) for x in arrays]


def pick_kernel(far_sends_ref, *refs):
    parts, refs = refs[:HEAD_DEVICES], refs[HEAD_DEVICES:]
    own_ref, out_refs, held_ref, sems = refs[0], refs[1 : 1 + LEVELS], refs[-4], refs[-3]
    index, sends_ref = sends_load(far_sends_ref, *refs[-2:])
    me = lax.axis_index("head")
    mine = OWN // HEAD_DEVICES
    copies = []
    for t, (steps, core) in enumerate(OFFSETS):
        source = offset_index(me, HEAD_DEVICES // 2 - steps, core)
        at = pl.ds(pl.multiple_of(source * mine, mine), mine)
        copies.append(pltpu.make_async_copy(parts[t], own_ref.at[at, :], sems.at[t]))
        copies[-1].start()
        held_ref[at, :] = parts[t][...]
    index.wait()
    for b in range(LEVELS):
        for s in range(SEND):
            out_refs[b][s * BLK : (s + 1) * BLK, :] = held_ref[rows_of(sends_ref[b, s]), :]
    for copy in copies:
        copy.wait()


def pick(sends, parts):
    return pl.pallas_call(
        pick_kernel,
        out_shape=[pltpu.HBM((OWN, 2 * WIDE), BF16)] + [pltpu.VMEM((PART, 2 * WIDE), BF16)] * LEVELS,
        in_specs=[HB] + [VM] * HEAD_DEVICES,
        out_specs=[HB] + [VM] * LEVELS,
        scratch_shapes=[pltpu.VMEM((OWN, 2 * WIDE), BF16), pltpu.SemaphoreType.DMA((HEAD_DEVICES,))]
        + sends_scratch(sends),
        compiler_params=limits(8),
        cost_estimate=pl.CostEstimate(flops=0, bytes_accessed=4 * 2**20, transcendentals=0),
        name="pick_boundary",
    )(*in_hbm(sends), *parts)


def staged_block(i, live, at, far, q_ref, g_ref, own_ref, acc_ref, staged, outs):
    rows = rows_of(i)
    q = q_ref[rows, :] * jnp.array(HD**-0.5, BF16)
    g = g_ref[rows, :]
    low = lax.broadcasted_iota(jnp.int32, (BLK, WIDE), 1) < HD
    z = jnp.zeros((BLK, WIDE), BF16)
    q = jnp.concatenate([jnp.where(low, q, z), jnp.where(low, z, q)], 0)
    g = jnp.concatenate([jnp.where(low, g, z), jnp.where(low, z, g)], 0)
    blocks = [own_ref[a, :] if a is not None else far[0][...] for a in at]
    kv = jnp.concatenate(blocks, 0)
    product = functools.partial(lax.dot_general, preferred_element_type=F32)
    across, plain, down = (((1,), (1,)), ((), ())), (((1,), (0,)), ((), ())), (((0,), (0,)), ((), ()))
    s = product(kv[:, :WIDE], q, across)
    d = product(kv[:, WIDE:], g, across)
    yield
    s = [s[j * BLK : (j + 1) * BLK] for j in range(NNB)]
    d = [d[j * BLK : (j + 1) * BLK] for j in range(NNB)]
    s[-1] = jnp.where(live, s[-1], FILL)
    peak = jnp.max(functools.reduce(jnp.maximum, s), 0, keepdims=True)
    p = [jnp.exp(x - peak) for x in s]
    total = jnp.sum(sum(p[1:], p[0]), 0, keepdims=True)
    dot = [x * y for x, y in zip(p, d)]
    inv = 1.0 / total
    dot = jnp.sum(sum(dot[1:], dot[0]), 0, keepdims=True) * inv
    weights = [x * inv for x in p]
    rounded = jnp.concatenate([x.astype(BF16) for x in weights], 0)
    grads = jnp.concatenate([(x * (y - dot)).astype(BF16) for x, y in zip(weights, d)], 0)
    yield
    terms = jnp.concatenate([product(grads, q, plain), product(rounded, g, plain)], 1)
    for j in range(NNB):
        term = terms[j * BLK : (j + 1) * BLK]
        if at[j] is None:
            far[1][...] = term.astype(BF16)
        else:
            acc_ref[at[j], :] += term
    yield
    results = product(jnp.concatenate([grads, rounded], 1), kv, down)
    qg, att = results[:WIDE, :WIDE], results[WIDE:, WIDE:]
    staged[0][rows, :] = jnp.where(low, att[:BLK], att[BLK:]).astype(BF16)
    staged[1][rows, :] = (jnp.where(low, qg[:BLK], qg[BLK:]) * HD**-0.5).astype(BF16)
    for copy in outs(i):
        copy.start()
    yield


def run_staged(blocks, ready=None):
    stages = 4
    for t in range(len(blocks) + stages - 1):
        for k in reversed(range(stages)):
            if 0 <= t - k < len(blocks):
                next(blocks[t - k])
                if ready and k == 2 and t - k in ready:
                    ready[t - k].start()


def row_copies(at, staged, outs, sems):
    return [
        pltpu.make_async_copy(x.at[rows_of(at), :], y.at[rows_of(at), :], sems.at[n, at])
        for n, (x, y) in enumerate(zip(staged, outs))
    ]


def inner_kernel(unroll, far_rows_ref, far_counts_ref, q_ref, far_g_ref, far_own_ref, *refs):
    att_ref, qg_ref, acc_ref, own_ref, g_ref, list_ref = refs[:6]
    staged, sems, in_sems = refs[6:8], refs[8], refs[9]
    rows_held, counts_held, index_sems = refs[10:]
    rows_index, rows_ref = rows_load(far_rows_ref, rows_held, index_sems.at[0])
    counts_index, counts_ref = counts_load(far_counts_ref, counts_held, index_sems.at[1])
    indices = [rows_index, counts_index]
    loads = []
    for n, (x, y) in enumerate(((far_own_ref, own_ref), (far_g_ref, g_ref))):
        for c in range(CHUNKS):
            part = pl.ds(c * (OWN // CHUNKS), OWN // CHUNKS)
            loads.append(pltpu.make_async_copy(x.at[part, :], y.at[part, :], in_sems.at[n, c]))
            loads[-1].start()
    outs = lambda i: row_copies(i, staged, (att_ref, qg_ref), sems)
    steps = NBLK - LEVELS * SEND
    acc_ref[...] = jnp.zeros_like(acc_ref)

    for load in indices:
        load.wait()

    def note(i, count):
        list_ref[count] = i
        return count + (rows_ref[i, 1] < NBLK).astype(jnp.int32)

    lax.fori_loop(0, NBLK, note, jnp.int32(0))
    for load in loads:
        load.wait()

    def step(t, carry):
        blocks = []
        for u in range(unroll):
            i = list_ref[t * unroll + u]
            at = [rows_of(rows_ref[i, j]) for j in range(NNB)]
            live = counts_ref[i] > NNB - 1
            blocks.append(staged_block(i, live, at, None, q_ref, g_ref, own_ref, acc_ref, staged, outs))
        run_staged(blocks)
        return carry

    lax.fori_loop(0, steps // unroll, step, 0)

    def settle(t, carry):
        for copy in outs(list_ref[t]):
            copy.wait()
        return carry

    lax.fori_loop(0, steps, settle, 0)


def inner(rows, counts, q, g, own):
    return pl.pallas_call(
        functools.partial(inner_kernel, 12),
        out_shape=[
            pltpu.HBM((OWN, WIDE), BF16),
            pltpu.HBM((OWN, WIDE), BF16),
            pltpu.VMEM((OWN, 2 * WIDE), F32),
            pltpu.VMEM((OWN, 2 * WIDE), BF16),
            pltpu.VMEM((OWN, WIDE), BF16),
        ],
        in_specs=[HB, HB, VM, HB, HB],
        out_specs=[HB, HB, VM, VM, VM],
        scratch_shapes=[pltpu.SMEM((NBLK + 1,), jnp.int32)]
        + [pltpu.VMEM((OWN, WIDE), BF16)] * 2
        + [pltpu.SemaphoreType.DMA((2, NBLK)), pltpu.SemaphoreType.DMA((2, CHUNKS))]
        + block_scratch(counts),
        compiler_params=limits(16),
        cost_estimate=pl.CostEstimate(flops=4 * 10**9, bytes_accessed=8 * 2**20, transcendentals=10**6),
        name="attend_inner",
    )(*in_hbm(rows, counts), q, *in_hbm(g, own))


def outer_kernel(levels, far_sends_ref, far_rows_ref, far_counts_ref, q_ref, g_ref, own_ref, *refs):
    recv_refs, refs = refs[: len(levels)], refs[len(levels) + 3 :]
    sends_held, sends_sem, rows_held, counts_held, index_sems = refs[-5:]
    refs = refs[:-5]
    sends_index, sends_ref = sends_load(far_sends_ref, sends_held, sends_sem)
    rows_index, rows_ref = rows_load(far_rows_ref, rows_held, index_sems.at[0])
    counts_index, counts_ref = counts_load(far_counts_ref, counts_held, index_sems.at[1])
    indices = [sends_index, rows_index, counts_index]
    for load in indices:
        load.wait()
    att_ref, qg_ref, acc_ref = refs[:3]
    back_refs, refs = refs[3 : 3 + len(levels)], refs[3 + len(levels) :]
    held, staged, sems, back_sems = refs[: len(levels)], refs[-4:-2], refs[-2], refs[-1]
    outs = lambda i: row_copies(i, staged, (att_ref, qg_ref), sems)
    backs = [pltpu.make_async_copy(x, y, back_sems.at[n]) for n, (x, y) in enumerate(zip(held, back_refs))]
    blocks, ready = [], {}
    for n, b in enumerate(levels):
        for s in range(SEND):
            i = sends_ref[b, s]
            at = [rows_of(rows_ref[i, j]) if j != 1 else None for j in range(NNB)]
            place = slice(s * BLK, (s + 1) * BLK)
            far = (recv_refs[n].at[place, :], held[n].at[place, :])
            live = counts_ref[i] > NNB - 1
            blocks.append(staged_block(i, live, at, far, q_ref, g_ref, own_ref, acc_ref, staged, outs))
        ready[len(blocks) - 1] = backs[n]
    run_staged(blocks, ready)
    for b in levels:
        for s in range(SEND):
            for copy in outs(sends_ref[b, s]):
                copy.wait()
    for copy in backs:
        copy.wait()


def outer(levels, sends, rows, counts, q, g, own, recv, done):
    recv = [recv[b] for b in levels]
    return pl.pallas_call(
        functools.partial(outer_kernel, levels),
        out_shape=[
            pltpu.HBM((OWN, WIDE), BF16),
            pltpu.HBM((OWN, WIDE), BF16),
            pltpu.VMEM((OWN, 2 * WIDE), F32),
        ]
        + [pltpu.HBM((PART, 2 * WIDE), BF16)] * len(levels),
        in_specs=[HB] * 3 + [VM] * (3 + len(levels)) + [HB, HB, VM],
        out_specs=[HB, HB, VM] + [HB] * len(levels),
        scratch_shapes=[pltpu.VMEM((PART, 2 * WIDE), BF16)] * len(levels)
        + [pltpu.VMEM((OWN, WIDE), BF16)] * 2
        + [pltpu.SemaphoreType.DMA((2, NBLK)), pltpu.SemaphoreType.DMA((len(levels),))]
        + sends_scratch(sends)
        + block_scratch(counts),
        input_output_aliases={6 + len(levels) + n: n for n in range(3)},
        compiler_params=limits(16),
        cost_estimate=pl.CostEstimate(flops=4 * 10**9, bytes_accessed=4 * 2**20, transcendentals=10**6),
        name="attend_outer",
    )(*in_hbm(sends, rows, counts), q, g, own, *recv, *done)


def join_kernel(far_sends_ref, acc_ref, *refs):
    index, sends_ref = sends_load(far_sends_ref, *refs[-2:])
    arrived_refs = refs[:LEVELS]
    key_ref, value_ref = refs[LEVELS : LEVELS + 2]
    key_ref[...] = acc_ref[:, :WIDE].astype(BF16)
    value_ref[...] = acc_ref[:, WIDE:].astype(BF16)
    index.wait()
    for b in range(LEVELS):
        for s in range(SEND):
            at = rows_of(sends_ref[b, s])
            both = acc_ref[at, :] + arrived_refs[b][s * BLK : (s + 1) * BLK, :].astype(F32)
            key_ref[at, :] = both[:, :WIDE].astype(BF16)
            value_ref[at, :] = both[:, WIDE:].astype(BF16)


def join(sends, acc, arrived):
    return pl.pallas_call(
        join_kernel,
        out_shape=[jax.ShapeDtypeStruct((OWN, WIDE), BF16)] * 2,
        in_specs=[HB] + [VM] * (1 + LEVELS),
        out_specs=[VM] * 2,
        scratch_shapes=sends_scratch(sends),
        compiler_params=limits(10),
        cost_estimate=pl.CostEstimate(flops=10**6, bytes_accessed=4 * 2**20, transcendentals=0),
        name="join_gradients",
    )(*in_hbm(sends), acc, *arrived)


def body(query_rows, key_rows, value_rows, out_grad, boundary_send_blocks, neighbours, live_count):
    heads = lax.axis_size("head")
    mine = query_rows.shape[0]
    sends, rows, counts = boundary_send_blocks.transpose(1, 2, 0), neighbours.T, live_count

    parts = split(key_rows, value_rows)
    parts = [shifted(x, *o) if o != (0, 0) else x for x, o in zip(parts, OFFSETS)]
    q = query_rows.reshape(mine, heads, WIDE).transpose(1, 0, 2)
    own, *outgoing = pick(sends, parts)
    q, own = lax.optimization_barrier((q, own))
    q = lax.all_to_all(q, "head", 0, 0, tiled=True).reshape(OWN, WIDE)
    recv = [swapped(outgoing[b], b) for b in range(LEVELS)]
    *done, own, grad = inner(rows, counts, q, out_grad, own)
    levels = tuple(range(LEVELS))
    attended, query_grad, acc, *back = outer(levels, sends, rows, counts, q, grad, own, recv, done)
    arrived = [swapped(back[b], b) for b in range(LEVELS)]
    attended = lax.all_to_all(attended.reshape(heads, mine, WIDE), "head", 0, 0, tiled=True)
    attended = attended.transpose(1, 0, 2).reshape(mine, heads * WIDE)
    attended, arrived[0] = lax.optimization_barrier((attended, arrived[0]))
    key_grad, value_grad = join(sends, acc, arrived)
    return attended, query_grad, key_grad, value_grad


def solution(mesh):
    rows = P(("pix", "head"), None)
    split = P("pix", "head")
    return jax.shard_map(
        body,
        mesh=mesh,
        in_specs=(rows, rows, rows, split, P(), P(), P()),
        out_specs=(rows, split, split, split),
        check_vma=False,
    )
```

```python
import functools
import jax
import jax.numpy as jnp
from jax import lax
from jax.experimental import pallas as pl
from jax.experimental.pallas import tpu as pltpu
from jax.sharding import PartitionSpec as P

HD = 64
BLK = 64
NNB = 9
NBLK = 32
LEVELS = 5
SEND = 4
WIDE = 2 * HD
OWN = NBLK * BLK
PART = SEND * BLK
FILL = -1e30
CHUNKS = 8
LANES = 128
FAR_FIRST = (2, 1, 4, 0, 3)
HEAD_DEVICES = 8
OFFSETS = ((1, 0), (3, 0), (1, 1), (3, 1), (2, 0), (2, 1), (0, 1), (0, 0))
F32 = jnp.float32
BF16 = jnp.bfloat16

VM = pl.BlockSpec(memory_space=pltpu.VMEM)
HB = pl.BlockSpec(memory_space=pltpu.HBM)


def swapped(block, bit):
    count = lax.axis_size("pix")
    route = [(low, low ^ (1 << bit)) for low in range(count)]
    return lax.ppermute(block, "pix", route)


def rows_of(start):
    return pl.ds(pl.multiple_of(start * BLK, BLK), BLK)


def offset_index(index, steps, core):
    chips = HEAD_DEVICES // 2
    return (index // 2 + steps) % chips * 2 + (index % 2 + core) % 2


def shifted(block, steps, core):
    route = [(i, offset_index(i, steps, core)) for i in range(HEAD_DEVICES)]
    return lax.ppermute(block, "head", route)


def limits(megabytes):
    return pltpu.CompilerParams(vmem_limit_bytes=megabytes * 2**20)


def split_kernel(key_ref, value_ref, *refs):
    parts, sems = refs[:-1], refs[-1]
    me = lax.axis_index("head")
    copies = []
    for t, (steps, core) in enumerate(OFFSETS):
        column = pl.ds(pl.multiple_of(offset_index(me, steps, core) * WIDE, WIDE), WIDE)
        for n, ref in enumerate((key_ref, value_ref)):
            copies.append(
                pltpu.make_async_copy(
                    ref.at[:, column], parts[t].at[:, n * WIDE : (n + 1) * WIDE], sems.at[2 * t + n]
                )
            )
    for copy in copies:
        copy.start()
    for copy in copies:
        copy.wait()


def split(keys, values):
    mine = keys.shape[0]
    return pl.pallas_call(
        split_kernel,
        out_shape=[pltpu.VMEM((mine, 2 * WIDE), BF16)] * HEAD_DEVICES,
        in_specs=[HB] * 2,
        out_specs=[VM] * HEAD_DEVICES,
        scratch_shapes=[pltpu.SemaphoreType.DMA((2 * HEAD_DEVICES,))],
        compiler_params=limits(4),
        cost_estimate=pl.CostEstimate(flops=0, bytes_accessed=2 * 2**20, transcendentals=0),
        name="split_keys_values",
    )(pltpu.with_memory_space_constraint(keys, pltpu.HBM), pltpu.with_memory_space_constraint(values, pltpu.HBM))


class Table:
    def __init__(self, ref, place):
        self.ref, self.place = ref, place

    def __getitem__(self, index):
        return self.ref[self.place(*index) if isinstance(index, tuple) else self.place(index)]


def sends_load(whole_ref, held_ref, sem):
    load = pltpu.make_async_copy(whole_ref, held_ref, sem)
    load.start()
    mine = lax.axis_index("pix")
    return load, Table(held_ref, lambda b, s: (b, s, mine))


def rows_load(whole_ref, held_ref, sem):
    mine = lax.axis_index("pix")
    per = LANES // NBLK
    columns = pl.ds(pl.multiple_of(mine // per * LANES, LANES), LANES)
    load = pltpu.make_async_copy(whole_ref.at[:, columns], held_ref, sem)
    load.start()
    return load, Table(held_ref, lambda i, j: (j, mine % per * NBLK + i))


def counts_load(whole_ref, held_ref, sem):
    load = pltpu.make_async_copy(whole_ref, held_ref, sem)
    load.start()
    mine = lax.axis_index("pix")
    return load, Table(held_ref, lambda i: mine * NBLK + i)


def sends_scratch(sends):
    return [pltpu.SMEM(sends.shape, jnp.int32), pltpu.SemaphoreType.DMA]


def block_scratch(counts):
    return [
        pltpu.SMEM((NNB, LANES), jnp.int32),
        pltpu.SMEM(counts.shape, jnp.int32),
        pltpu.SemaphoreType.DMA((2,)),
    ]


def in_hbm(*arrays):
    return [pltpu.with_memory_space_constraint(x, pltpu.HBM) for x in arrays]


def pick_kernel(far_sends_ref, *refs):
    parts, refs = refs[:HEAD_DEVICES], refs[HEAD_DEVICES:]
    own_ref, out_refs, held_ref, sems = refs[0], refs[1 : 1 + LEVELS], refs[-4], refs[-3]
    index, sends_ref = sends_load(far_sends_ref, *refs[-2:])
    me = lax.axis_index("head")
    mine = OWN // HEAD_DEVICES
    copies = []
    for t, (steps, core) in enumerate(OFFSETS):
        source = offset_index(me, HEAD_DEVICES // 2 - steps, core)
        at = pl.ds(pl.multiple_of(source * mine, mine), mine)
        copies.append(pltpu.make_async_copy(parts[t], own_ref.at[at, :], sems.at[t]))
        copies[-1].start()
        held_ref[at, :] = parts[t][...]
    index.wait()
    for b in range(LEVELS):
        for s in range(SEND):
            out_refs[b][s * BLK : (s + 1) * BLK, :] = held_ref[rows_of(sends_ref[b, s]), :]
    for copy in copies:
        copy.wait()


def pick(sends, parts):
    return pl.pallas_call(
        pick_kernel,
        out_shape=[pltpu.HBM((OWN, 2 * WIDE), BF16)] + [pltpu.VMEM((PART, 2 * WIDE), BF16)] * LEVELS,
        in_specs=[HB] + [VM] * HEAD_DEVICES,
        out_specs=[HB] + [VM] * LEVELS,
        scratch_shapes=[pltpu.VMEM((OWN, 2 * WIDE), BF16), pltpu.SemaphoreType.DMA((HEAD_DEVICES,))]
        + sends_scratch(sends),
        compiler_params=limits(8),
        cost_estimate=pl.CostEstimate(flops=0, bytes_accessed=4 * 2**20, transcendentals=0),
        name="pick_boundary",
    )(*in_hbm(sends), *parts)


def staged_block(i, live, at, far, q_ref, g_ref, own_ref, acc_ref, staged, outs):
    rows = rows_of(i)
    q = q_ref[rows, :] * jnp.array(HD**-0.5, BF16)
    g = g_ref[rows, :]
    low = lax.broadcasted_iota(jnp.int32, (BLK, WIDE), 1) < HD
    z = jnp.zeros((BLK, WIDE), BF16)
    q = jnp.concatenate([jnp.where(low, q, z), jnp.where(low, z, q)], 0)
    g = jnp.concatenate([jnp.where(low, g, z), jnp.where(low, z, g)], 0)
    blocks = [own_ref[a, :] if a is not None else far[0][...] for a in at]
    kv = jnp.concatenate(blocks, 0)
    product = functools.partial(lax.dot_general, preferred_element_type=F32)
    across, plain, down = (((1,), (1,)), ((), ())), (((1,), (0,)), ((), ())), (((0,), (0,)), ((), ()))
    s = product(kv[:, :WIDE], q, across)
    d = product(kv[:, WIDE:], g, across)
    yield
    s = [s[j * BLK : (j + 1) * BLK] for j in range(NNB)]
    d = [d[j * BLK : (j + 1) * BLK] for j in range(NNB)]
    s[-1] = jnp.where(live, s[-1], FILL)
    peak = jnp.max(functools.reduce(jnp.maximum, s), 0, keepdims=True)
    p = [jnp.exp(x - peak) for x in s]
    total = jnp.sum(sum(p[1:], p[0]), 0, keepdims=True)
    dot = [x * y for x, y in zip(p, d)]
    inv = 1.0 / total
    dot = jnp.sum(sum(dot[1:], dot[0]), 0, keepdims=True) * inv
    weights = [x * inv for x in p]
    rounded = jnp.concatenate([x.astype(BF16) for x in weights], 0)
    grads = jnp.concatenate([(x * (y - dot)).astype(BF16) for x, y in zip(weights, d)], 0)
    yield
    terms = jnp.concatenate([product(grads, q, plain), product(rounded, g, plain)], 1)
    for j in range(NNB):
        term = terms[j * BLK : (j + 1) * BLK]
        if at[j] is None:
            far[1][...] = term.astype(BF16)
        else:
            acc_ref[at[j], :] += term
    yield
    results = product(jnp.concatenate([grads, rounded], 1), kv, down)
    qg, att = results[:WIDE, :WIDE], results[WIDE:, WIDE:]
    staged[0][rows, :] = jnp.where(low, att[:BLK], att[BLK:]).astype(BF16)
    staged[1][rows, :] = (jnp.where(low, qg[:BLK], qg[BLK:]) * HD**-0.5).astype(BF16)
    for copy in outs(i):
        copy.start()
    yield


def run_staged(blocks, ready=None):
    stages = 4
    for t in range(len(blocks) + stages - 1):
        for k in reversed(range(stages)):
            if 0 <= t - k < len(blocks):
                next(blocks[t - k])
                if ready and k == 2 and t - k in ready:
                    ready[t - k].start()


def row_copies(at, staged, outs, sems):
    return [
        pltpu.make_async_copy(x.at[rows_of(at), :], y.at[rows_of(at), :], sems.at[n, at])
        for n, (x, y) in enumerate(zip(staged, outs))
    ]


def inner_kernel(unroll, far_rows_ref, far_counts_ref, q_ref, far_g_ref, far_own_ref, *refs):
    att_ref, qg_ref, acc_ref, own_ref, g_ref, list_ref = refs[:6]
    staged, sems, in_sems = refs[6:8], refs[8], refs[9]
    rows_held, counts_held, index_sems = refs[10:]
    rows_index, rows_ref = rows_load(far_rows_ref, rows_held, index_sems.at[0])
    counts_index, counts_ref = counts_load(far_counts_ref, counts_held, index_sems.at[1])
    indices = [rows_index, counts_index]
    loads = []
    for n, (x, y) in enumerate(((far_own_ref, own_ref), (far_g_ref, g_ref))):
        for c in range(CHUNKS):
            part = pl.ds(c * (OWN // CHUNKS), OWN // CHUNKS)
            loads.append(pltpu.make_async_copy(x.at[part, :], y.at[part, :], in_sems.at[n, c]))
            loads[-1].start()
    outs = lambda i: row_copies(i, staged, (att_ref, qg_ref), sems)
    steps = NBLK - LEVELS * SEND
    acc_ref[...] = jnp.zeros_like(acc_ref)

    for load in indices:
        load.wait()

    def note(i, count):
        list_ref[count] = i
        return count + (rows_ref[i, 1] < NBLK).astype(jnp.int32)

    lax.fori_loop(0, NBLK, note, jnp.int32(0))
    for load in loads:
        load.wait()

    def step(t, carry):
        blocks = []
        for u in range(unroll):
            i = list_ref[t * unroll + u]
            at = [rows_of(rows_ref[i, j]) for j in range(NNB)]
            live = counts_ref[i] > NNB - 1
            blocks.append(staged_block(i, live, at, None, q_ref, g_ref, own_ref, acc_ref, staged, outs))
        run_staged(blocks)
        return carry

    lax.fori_loop(0, steps // unroll, step, 0)

    def settle(t, carry):
        for copy in outs(list_ref[t]):
            copy.wait()
        return carry

    lax.fori_loop(0, steps, settle, 0)


def inner(rows, counts, q, g, own):
    return pl.pallas_call(
        functools.partial(inner_kernel, 12),
        out_shape=[
            pltpu.HBM((OWN, WIDE), BF16),
            pltpu.HBM((OWN, WIDE), BF16),
            pltpu.VMEM((OWN, 2 * WIDE), F32),
            pltpu.VMEM((OWN, 2 * WIDE), BF16),
            pltpu.VMEM((OWN, WIDE), BF16),
        ],
        in_specs=[HB, HB, VM, HB, HB],
        out_specs=[HB, HB, VM, VM, VM],
        scratch_shapes=[pltpu.SMEM((NBLK + 1,), jnp.int32)]
        + [pltpu.VMEM((OWN, WIDE), BF16)] * 2
        + [pltpu.SemaphoreType.DMA((2, NBLK)), pltpu.SemaphoreType.DMA((2, CHUNKS))]
        + block_scratch(counts),
        compiler_params=limits(16),
        cost_estimate=pl.CostEstimate(flops=4 * 10**9, bytes_accessed=8 * 2**20, transcendentals=10**6),
        name="attend_inner",
    )(*in_hbm(rows, counts), q, *in_hbm(g, own))


def outer_kernel(levels, far_sends_ref, far_rows_ref, far_counts_ref, q_ref, g_ref, own_ref, *refs):
    recv_refs, refs = refs[: len(levels)], refs[len(levels) + 3 :]
    sends_held, sends_sem, rows_held, counts_held, index_sems = refs[-5:]
    refs = refs[:-5]
    sends_index, sends_ref = sends_load(far_sends_ref, sends_held, sends_sem)
    rows_index, rows_ref = rows_load(far_rows_ref, rows_held, index_sems.at[0])
    counts_index, counts_ref = counts_load(far_counts_ref, counts_held, index_sems.at[1])
    indices = [sends_index, rows_index, counts_index]
    for load in indices:
        load.wait()
    att_ref, qg_ref, acc_ref = refs[:3]
    back_refs, refs = refs[3 : 3 + len(levels)], refs[3 + len(levels) :]
    held, staged, sems, back_sems = refs[: len(levels)], refs[-4:-2], refs[-2], refs[-1]
    outs = lambda i: row_copies(i, staged, (att_ref, qg_ref), sems)
    backs = [pltpu.make_async_copy(x, y, back_sems.at[n]) for n, (x, y) in enumerate(zip(held, back_refs))]
    blocks, ready = [], {}
    for n, b in enumerate(levels):
        for s in range(SEND):
            i = sends_ref[b, s]
            at = [rows_of(rows_ref[i, j]) if j != 1 else None for j in range(NNB)]
            place = slice(s * BLK, (s + 1) * BLK)
            far = (recv_refs[n].at[place, :], held[n].at[place, :])
            live = counts_ref[i] > NNB - 1
            blocks.append(staged_block(i, live, at, far, q_ref, g_ref, own_ref, acc_ref, staged, outs))
        ready[len(blocks) - 1] = backs[n]
    run_staged(blocks, ready)
    for b in levels:
        for s in range(SEND):
            for copy in outs(sends_ref[b, s]):
                copy.wait()
    for copy in backs:
        copy.wait()


def outer(levels, sends, rows, counts, q, g, own, recv, done):
    recv = [recv[b] for b in levels]
    return pl.pallas_call(
        functools.partial(outer_kernel, levels),
        out_shape=[
            pltpu.HBM((OWN, WIDE), BF16),
            pltpu.HBM((OWN, WIDE), BF16),
            pltpu.VMEM((OWN, 2 * WIDE), F32),
        ]
        + [pltpu.HBM((PART, 2 * WIDE), BF16)] * len(levels),
        in_specs=[HB] * 3 + [VM] * (3 + len(levels)) + [HB, HB, VM],
        out_specs=[HB, HB, VM] + [HB] * len(levels),
        scratch_shapes=[pltpu.VMEM((PART, 2 * WIDE), BF16)] * len(levels)
        + [pltpu.VMEM((OWN, WIDE), BF16)] * 2
        + [pltpu.SemaphoreType.DMA((2, NBLK)), pltpu.SemaphoreType.DMA((len(levels),))]
        + sends_scratch(sends)
        + block_scratch(counts),
        input_output_aliases={6 + len(levels) + n: n for n in range(3)},
        compiler_params=limits(16),
        cost_estimate=pl.CostEstimate(flops=4 * 10**9, bytes_accessed=4 * 2**20, transcendentals=10**6),
        name="attend_outer",
    )(*in_hbm(sends, rows, counts), q, g, own, *recv, *done)


def join_kernel(far_sends_ref, acc_ref, *refs):
    index, sends_ref = sends_load(far_sends_ref, *refs[-2:])
    arrived_refs = refs[:LEVELS]
    key_ref, value_ref = refs[LEVELS : LEVELS + 2]
    key_ref[...] = acc_ref[:, :WIDE].astype(BF16)
    value_ref[...] = acc_ref[:, WIDE:].astype(BF16)
    index.wait()
    for n, b in enumerate(FAR_FIRST):
        for s in range(SEND):
            at = rows_of(sends_ref[b, s])
            both = acc_ref[at, :] + arrived_refs[n][s * BLK : (s + 1) * BLK, :].astype(F32)
            key_ref[at, :] = both[:, :WIDE].astype(BF16)
            value_ref[at, :] = both[:, WIDE:].astype(BF16)


def join(sends, acc, arrived):
    return pl.pallas_call(
        join_kernel,
        out_shape=[jax.ShapeDtypeStruct((OWN, WIDE), BF16)] * 2,
        in_specs=[HB] + [VM] * (1 + LEVELS),
        out_specs=[VM] * 2,
        scratch_shapes=sends_scratch(sends),
        compiler_params=limits(10),
        cost_estimate=pl.CostEstimate(flops=10**6, bytes_accessed=4 * 2**20, transcendentals=0),
        name="join_gradients",
    )(*in_hbm(sends), acc, *arrived)


def body(query_rows, key_rows, value_rows, out_grad, boundary_send_blocks, neighbours, live_count):
    heads = lax.axis_size("head")
    mine = query_rows.shape[0]
    sends, rows, counts = boundary_send_blocks.transpose(1, 2, 0), neighbours.T, live_count

    parts = split(key_rows, value_rows)
    parts = [shifted(x, *o) if o != (0, 0) else x for x, o in zip(parts, OFFSETS)]
    q = query_rows.reshape(mine, heads, WIDE).transpose(1, 0, 2)
    own, *outgoing = pick(sends, parts)
    q, own = lax.optimization_barrier((q, own))
    q = lax.all_to_all(q, "head", 0, 0, tiled=True).reshape(OWN, WIDE)
    recv = [swapped(outgoing[b], b) for b in range(LEVELS)]
    *done, own, grad = inner(rows, counts, q, out_grad, own)
    attended, query_grad, acc, *back = outer(FAR_FIRST, sends, rows, counts, q, grad, own, recv, done)
    arrived = [swapped(x, b) for x, b in zip(back, FAR_FIRST)]
    attended = lax.all_to_all(attended.reshape(heads, mine, WIDE), "head", 0, 0, tiled=True)
    attended = attended.transpose(1, 0, 2).reshape(mine, heads * WIDE)
    attended, arrived[0] = lax.optimization_barrier((attended, arrived[0]))
    key_grad, value_grad = join(sends, acc, arrived)
    return attended, query_grad, key_grad, value_grad


def solution(mesh):
    rows = P(("pix", "head"), None)
    split = P("pix", "head")
    return jax.shard_map(
        body,
        mesh=mesh,
        in_specs=(rows, rows, rows, split, P(), P(), P()),
        out_specs=(rows, split, split, split),
        check_vma=False,
    )
```
